512 devices in a mesh: vir: 64 (over x, z_hi, y), occ: 8 (over z_lo, core).
Axes of the slice: x: 4, y: 8, z: 8 (z_hi: 2, z_lo: 4; z = z_hi * 4 + z_lo), core: 2. Of those that a mesh axis runs over, the one named last changes fastest.
Arguments:
- triple_amps: bfloat16 [64, 4096, 512], P('vir', 'occ'), may hold values from -6 to 6
- double_amps: bfloat16 [64, 96, 512], P('vir'), may hold values from -6 to 6
- ladder_block_table: bfloat16 [64, 6, 512, 512], P('vir'), may hold values from -0.109375 to 0.109375
- source_ids: int32 [64, 6], replicated, may hold values from 0 to 63
- list_length: int32 [64], replicated, may hold values from 1 to 6, 192 in all
- partner: int32 [64], replicated, may hold values from 0 to 63, as said below
- virtual_energy: float32 [64, 512], P('vir'), may hold values from 0.5 to 3
- triple_occupied_energy: float32 [4096], P('occ'), may hold values from -3 to -0.3
- coupling: bfloat16 [4096, 96], P('occ'), may hold values from -0.625 to 0.625
- projector: bfloat16 [4096, 96], P('occ'), may hold values from -0.09375 to 0.09375
Outputs:
- sigma_triples: bfloat16 [64, 4096, 512], P('vir', 'occ')
- sigma_doubles: float32 [64, 96, 512], P('vir', 'occ')
The draws below stay inside these ranges and needn't reach their ends.
Inputs may be any that keep to these rules, and one draw needn't show every extreme that they name: partner pairs the tiles: partner[partner[p]] = p and partner[p] != p.
All inputs are finite; a program needn't handle non-finite values.
Results may differ from the reference program's by a relative error of at most 0.007.
Values may be sent and summed in bfloat16 or wider, within the bound.
A program may use at most 64 MiB of HBM per device.

```python
import math
import jax
import jax.numpy as jnp
import numpy as np
from jax import lax

VPAIR = 512
OCCJ = 96
LIST = 6
TILES = 64
ROWS = 4096


def draw_partner(key, part):
    key = jax.random.fold_in(key, 5)
    order = jax.random.permutation(key, TILES).astype(jnp.int32)
    first = order[0::2]
    second = order[1::2]
    paired = jnp.zeros((TILES,), jnp.int32).at[first].set(second)
    return paired.at[second].set(first)


def set_ends(entries, stream_key, smallest, largest):
    longest = entries.shape.index(max(entries.shape))
    spots = []
    for shift in (0, 1):
        where = [jax.random.randint(jax.random.fold_in(stream_key, axis), (), 0, length) for axis, length in enumerate(entries.shape)]
        where[longest] = (where[longest] + shift) % entries.shape[longest]
        spots.append(tuple(where))
    return entries.at[spots[0]].set(smallest).at[spots[1]].set(largest)


def block_levels(stream_key, shape, shards, low, top_value):
    def one(position, shards_of):
        draws = jax.random.uniform(jax.random.fold_in(jax.random.fold_in(stream_key, 6), position), (shards_of,), jnp.float32, low / len(shards), top_value / len(shards))
        return jnp.repeat(jnp.exp(draws), shape[position] // shards_of).reshape((-1,) + (1,) * (len(shape) - position - 1))

    loudness = one(*shards[0])
    for cut in shards[1:]:
        loudness = loudness * one(*cut)
    return loudness


def profile(count, total, reach, lean):
    portions = [(1 << 20) // math.isqrt(grade ** lean) + 1 for grade in range(2, count + 1)]
    rest, given = total - reach - (count - 1), [1] * (count - 1)
    while rest > 0:
        movable = [i for i in range(count - 1) if given[i] < reach]
        mass, budget = sum([portions[i] for i in movable]), rest
        for i in movable:
            extra = min(reach - given[i], max(1, budget * portions[i] // mass), rest)
            given[i] = given[i] + extra
            rest = rest - extra
    return np.array([reach] + given)


def ragged_sizes(key, amount, total, most, slope):
    if amount == 2:
        one = jax.random.randint(key, (), max(1, total - most), min(most, total - 1) + 1)
        return jnp.stack([one, total - one])
    sizes = jnp.asarray(profile(amount, total, most, slope), jnp.int32)
    couples = (amount - 1) // 2
    giver, receiver = sizes[1:1 + 2 * couples:2], sizes[2:2 + 2 * couples:2]
    room = jnp.minimum(giver - 1, most - receiver)
    passed = jax.random.randint(jax.random.fold_in(key, 1), (couples,), 0, 1 << 20) % (room + 1)
    sizes = sizes.at[1:1 + 2 * couples:2].set(giver - passed).at[2:2 + 2 * couples:2].set(receiver + passed)
    return sizes[jax.random.permutation(jax.random.fold_in(key, 2), amount)]


def scatter_about(own_key, shape, width, limit, shards=(), kind=jnp.bfloat16):
    entries = jax.random.normal(own_key, shape, jnp.float32) * width
    if len(shards) > 0:
        entries = block_levels(own_key, shape, shards, -0.22, 0.18) * entries
    return jnp.clip(entries, min=-limit, max=limit).astype(kind)


def setup_inputs(seed: int = 0) -> dict:
    key_list = jax.random.split(jax.random.key(seed), 11)
    return {
        "triple_amps": scatter_about(key_list[0], (TILES, ROWS, VPAIR), 1.0, 6.0, ((0, 64), (1, 8))),
        "double_amps": scatter_about(key_list[1], (TILES, OCCJ, VPAIR), 1.0, 6.0, ((0, 64),)),
        "ladder_block_table": scatter_about(key_list[2], (TILES, LIST, VPAIR, VPAIR), (VPAIR * LIST) ** -0.5, 0.109375, ((0, 64),)),
        "source_ids": set_ends(jax.random.randint(key_list[3], (TILES, LIST), 0, TILES), jax.random.fold_in(key_list[3], 1), 0, TILES - 1).astype(jnp.int32),
        "list_length": ragged_sizes(key_list[4], TILES, TILES * LIST // 2, LIST, 2).astype(jnp.int32),
        "partner": draw_partner(jax.random.fold_in(key_list[10], 71), 0),
        "virtual_energy": jnp.clip(0.5 + 2.5 * jax.random.uniform(key_list[6], (TILES, VPAIR), jnp.float32) ** block_levels(key_list[6], (TILES, VPAIR), ((0, 64),), -0.2, 0.2), 0.5, 3.0),
        "triple_occupied_energy": jnp.clip(-3.0 + 2.7 * jax.random.uniform(key_list[7], (ROWS,), jnp.float32) ** block_levels(key_list[7], (ROWS,), ((0, 8),), -0.2, 0.2), -3.0, -0.3),
        "coupling": scatter_about(key_list[8], (ROWS, OCCJ), OCCJ ** -0.5, 0.625, ((0, 8),)),
        "projector": scatter_about(key_list[9], (ROWS, OCCJ), ROWS ** -0.5, 0.09375, ((0, 8),)),
    }


def reference(triple_amps, double_amps, ladder_block_table, source_ids, list_length, partner, virtual_energy, triple_occupied_energy, coupling, projector):
    slots = jnp.arange(LIST, dtype=jnp.int32)

    def one_tile(tile):
        ids = source_ids[tile]
        others = partner[ids]
        live = (slots < list_length[tile]).astype(jnp.float32)
        differ = triple_amps[ids].astype(jnp.float32) - triple_amps[others].astype(jnp.float32)
        source_tile = (differ * live[:, None, None]).astype(jnp.bfloat16)
        terms = jnp.einsum("lre,lef->lrf", source_tile.astype(jnp.float32), ladder_block_table[tile].astype(jnp.float32))
        ladder_integral = jnp.sum(terms, axis=0)
        fock = (virtual_energy[tile][None, :] - triple_occupied_energy[:, None]) * triple_amps[tile].astype(jnp.float32)
        couple = jnp.dot(coupling, double_amps[tile], preferred_element_type=jnp.float32)
        total_block = ladder_integral + fock + couple
        sigma_triple_block = total_block.astype(jnp.bfloat16)
        sigma_two = jnp.dot(projector.astype(jnp.float32).T, total_block, preferred_element_type=jnp.float32)
        return sigma_triple_block, sigma_two

    sigma_triples, sigma_doubles = lax.map(one_tile, jnp.arange(TILES, dtype=jnp.int32))
    return sigma_triples, sigma_doubles
```

```python
import jax
import jax.numpy as jnp
from jax import lax
from jax.experimental import pallas as pl
from jax.experimental.pallas import tpu as pltpu
from jax.sharding import PartitionSpec as P

MESH = pl.DeviceIdType.MESH

NX, NZ, NY, NO = 4, 2, 8, 8
TILES = NX * NZ * NY
PAIRS = TILES // 2
SLOTS = 6
ROWS = 512
COLS = 512
BLOCK = ROWS // (NX * NY)
HALF = COLS // NZ
OCCJ = 96
SHARE = OCCJ // NO
PAD = 16
OFFSETS = (0, -1, 1, -2, 2, -3, 3, 4)
NEAR = 7 * NX * BLOCK


def kernel(
    t_ref, da_ref, ladder_hbm, ids_ref, len_ref, partner_ref, ven_ref, occ_ref, coup_ref, proj_ref,
    out_ref, out2_ref,
    ladder, chunks, ring, picked, sources, acc, base, low, proj_t, part, got,
    rank, following, first, pick,
    ladder_sem, p1_send, p1_recv, own_sem, z_send, z_recv, y_send, y_recv, x_send, x_recv, o_send, o_recv,
):
    vir, occ = lax.axis_index("vir"), lax.axis_index("occ")
    x, zh, y = vir // (NZ * NY), (vir // NY) % NZ, vir % NY

    def vir_at(dx, dz, dy):
        return ((x + dx) % NX) * (NZ * NY) + ((zh + dz) % NZ) * NY + (y + dy) % NY

    def vir_off(j):
        return vir_at(j // (NZ * NY), (j // NY) % NZ, j % NY)

    get_ladder = pltpu.make_async_copy(ladder_hbm.at[0], ladder, ladder_sem)
    get_ladder.start()

    barrier = pltpu.get_barrier_semaphore()

    @pl.loop(1, TILES)
    def _(j):
        pl.semaphore_signal(barrier, inc=1, device_id=(vir_off(j), occ), device_id_type=MESH)

    @pl.loop(1, NO)
    def _(j):
        pl.semaphore_signal(barrier, inc=1, device_id=(vir, (occ + j) % NO), device_id_type=MESH)

    pl.semaphore_wait(barrier, TILES + NO - 2)

    def chunk_of(v):
        vx, vz, vy = v // (NZ * NY), (v // NY) % NZ, v % NY
        return t_ref.at[
            0,
            pl.ds(pl.multiple_of(vx * (NY * BLOCK) + vy * BLOCK, BLOCK), BLOCK),
            pl.ds(pl.multiple_of(vz * HALF, HALF), HALF),
        ]

    @pl.loop(1, TILES)
    def _(j):
        to = vir_off(j)
        pltpu.make_async_remote_copy(
            src_ref=chunk_of(to), dst_ref=chunks.at[vir], send_sem=p1_send, recv_sem=p1_recv,
            device_id=(to, occ), device_id_type=MESH,
        ).start()

    keep = pltpu.make_async_copy(chunk_of(vir), chunks.at[vir], own_sem)
    keep.start()

    @pl.loop(0, TILES)
    def _(t):
        rank[t] = 0

    def number(t, count):
        other = partner_ref[t]
        lower = t < other
        rank[t] = jnp.where(lower, count, rank[other])
        return count + lower.astype(jnp.int32)

    lax.fori_loop(0, TILES, number, jnp.int32(0))
    following[TILES] = 0

    def look_back(i, nxt):
        t = TILES - 1 - i
        nxt = jnp.where(t < partner_ref[t], t, nxt)
        following[t] = nxt
        return nxt

    lax.fori_loop(0, TILES, look_back, jnp.int32(0))

    def list_first(k, t):
        low_tile = following[t]
        first[k] = low_tile
        return low_tile + 1

    lax.fori_loop(0, PAIRS, list_first, jnp.int32(0))

    for j in range(NX):
        for l in range(SLOTS):
            pick[j * SLOTS + l] = rank[ids_ref[vir_at(j, 0, 0), l]]

    proj_t[...] = jnp.zeros_like(proj_t)
    flipped = proj_ref[...].astype(jnp.float32).T
    for o in range(NO):
        proj_t[PAD * o : PAD * o + SHARE, :] = flipped[SHARE * o : SHARE * (o + 1), :].astype(jnp.bfloat16)
    for i in range(ROWS // 128):
        rows = slice(128 * i, 128 * (i + 1))
        column = jnp.broadcast_to(occ_ref[:, rows], (128, 128)).T
        wide = jnp.concatenate([column] * (COLS // 128), axis=1)
        couple = jnp.dot(coup_ref[rows, :], da_ref[0], preferred_element_type=jnp.float32)
        base[rows, :] = couple + (ven_ref[...] - wide) * t_ref[0, rows, :].astype(jnp.float32)

    get_ladder.wait()
    for l in range(SLOTS):
        tile = ids_ref[vir, l]
        sign = jnp.where(tile < partner_ref[tile], 1.0, -1.0)
        factor = jnp.where(l < len_ref[vir], sign, 0.0).astype(jnp.float32)
        ladder[l] = (ladder[l].astype(jnp.float32) * factor).astype(jnp.bfloat16)

    keep.wait()
    arrived = chunks.at[0 : TILES - 1]
    pltpu.make_async_copy(arrived, arrived, p1_recv).wait()

    @pl.loop(0, PAIRS)
    def _(k):
        tile = first[k]
        ring[0][k] = (
            chunks[tile].astype(jnp.float32) - chunks[partner_ref[tile]].astype(jnp.float32)
        ).astype(jnp.bfloat16)

    sent = []

    def send(src, dst, send_sem, recv_sem, to):
        copy = pltpu.make_async_remote_copy(
            src_ref=src, dst_ref=dst, send_sem=send_sem, recv_sem=recv_sem, device_id=to, device_id_type=MESH
        )
        copy.start()
        return copy

    def arrival(dst, sem):
        pltpu.make_async_copy(dst, dst, sem).wait()

    up, down = (vir_at(0, 0, 1), occ), (vir_at(0, 0, -1), occ)

    def pass_on(h, step):
        mine = h * 8
        left = ring[mine] if step == 0 else ring[mine + 2 * step - 1]
        right = ring[mine] if step == 0 else ring[mine + 2 * step]
        i = h * 8 + 2 * step
        if step < 3:
            sent.append(send(left, ring[mine + 2 * step + 1], y_send.at[i], y_recv.at[i], up))
            sent.append(send(right, ring[mine + 2 * step + 2], y_send.at[i + 1], y_recv.at[i + 1], down))
        else:
            last, half = ring[mine + 7], PAIRS // 2
            sent.append(send(left.at[0:half], last.at[0:half], y_send.at[i], y_recv.at[i], up))
            sent.append(send(right.at[half:], last.at[half:], y_send.at[i + 1], y_recv.at[i + 1], down))

    def await_step(h, step):
        i = h * 8 + 2 * (step - 1)
        if step < 4:
            arrival(ring[h * 8 + 2 * step - 1], y_recv.at[i])
            arrival(ring[h * 8 + 2 * step], y_recv.at[i + 1])
        else:
            last, half = ring[h * 8 + 7], PAIRS // 2
            arrival(last.at[0:half], y_recv.at[i])
            arrival(last.at[half:], y_recv.at[i + 1])

    def deal(h, s):
        block, out = ring[h * 8 + s], picked[h * 8 + s]
        half = zh if h == 0 else 1 - zh
        where = pl.ds(pl.multiple_of(s * NX * BLOCK + x * BLOCK, BLOCK), BLOCK)
        for j in range(1, NX):
            for l in range(SLOTS):
                out[j - 1, l] = block[pick[j * SLOTS + l]]
            send(
                out.at[j - 1], sources.at[:, half, where, :], x_send.at[h * 8 + s], x_recv.at[h * 8 + s],
                (vir_at(j, 0, 0), occ),
            )
        for l in range(SLOTS):
            sources[l, half, where, :] = block[pick[l]]

    def deal_step(h, step):
        if step == 0:
            deal(h, 0)
        elif step == 4:
            deal(h, 7)
        else:
            deal(h, 2 * step - 1)
            deal(h, 2 * step)

    pass_on(0, 0)
    sent.append(send(ring[0], ring[8], z_send, z_recv, (vir_at(0, 1, 0), occ)))
    deal_step(0, 0)
    for h, step in ((0, 1), (1, 0), (0, 2), (1, 1), (0, 3), (1, 2), (0, 4), (1, 3), (1, 4)):
        if (h, step) == (1, 0):
            arrival(ring[8], z_recv)
        else:
            await_step(h, step)
        if step < 4:
            pass_on(h, step)
        deal_step(h, step)

    def multiply(begin, end):
        for s in range(8):
            if begin <= s * NX * BLOCK < end:
                for h in range(2):
                    arrival(picked[h * 8 + s], x_recv.at[h * 8 + s])
        acc[begin:end] = jnp.zeros((end - begin, COLS), jnp.float32)

        @pl.loop(0, SLOTS)
        def _(l):
            acc[begin:end] += jnp.dot(
                sources[l, 0, begin:end, :], ladder[l, 0:HALF, :], preferred_element_type=jnp.float32
            ) + jnp.dot(sources[l, 1, begin:end, :], ladder[l, HALF:COLS, :], preferred_element_type=jnp.float32)

        @pl.loop(begin // BLOCK, end // BLOCK)
        def _(b):
            s, bx = b // NX, b % NX
            offset = (s // 2) * (1 - s % 2) - ((s + 1) // 2) * (s % 2)
            rows = pl.ds(pl.multiple_of(bx * (NY * BLOCK) + ((y + offset + NY) % NY) * BLOCK, BLOCK), BLOCK)
            total = base[rows, :] + acc[pl.ds(pl.multiple_of(b * BLOCK, BLOCK), BLOCK), :]
            high = total.astype(jnp.bfloat16)
            out_ref[0, rows, :] = high
            low[rows, :] = (total - high.astype(jnp.float32)).astype(jnp.bfloat16)

    multiply(0, NEAR)
    multiply(NEAR, ROWS)

    both = jnp.dot(proj_t[...], out_ref[0], preferred_element_type=jnp.float32) + jnp.dot(
        proj_t[...], low[...], preferred_element_type=jnp.float32
    )
    for o in range(NO):
        part[o] = both[PAD * o : PAD * (o + 1), :].astype(jnp.bfloat16)

    @pl.loop(1, NO)
    def _(j):
        to = (occ + j) % NO
        send(part.at[to], got.at[j - 1], o_send, o_recv, (vir, to))

    arrival(got, o_recv)
    total = part[occ].astype(jnp.float32)
    for j in range(NO - 1):
        total = total + got[j].astype(jnp.float32)
    out2_ref[0] = total[0:SHARE, :]

    for copy in sent:
        copy.wait_send()
    pltpu.make_async_copy(arrived, arrived, p1_send).wait()
    for i in range(16):
        pltpu.make_async_copy(picked[i], picked[i], x_send.at[i]).wait()
    pltpu.make_async_copy(got, got, o_send).wait()


def on_device(
    triple_amps, double_amps, ladder_block_table, source_ids, list_length, partner, virtual_energy,
    triple_occupied_energy, coupling, projector,
):
    vmem, smem = pl.BlockSpec(memory_space=pltpu.VMEM), pl.BlockSpec(memory_space=pltpu.SMEM)
    bf16, f32 = jnp.bfloat16, jnp.float32
    dma = pltpu.SemaphoreType.DMA
    return pl.pallas_call(
        kernel,
        out_shape=(
            jax.ShapeDtypeStruct((1, ROWS, COLS), bf16),
            jax.ShapeDtypeStruct((1, SHARE, COLS), f32),
        ),
        in_specs=[vmem, vmem, pl.BlockSpec(memory_space=pl.ANY), smem, smem, smem, vmem, vmem, vmem, vmem],
        out_specs=(vmem, vmem),
        scratch_shapes=[
            pltpu.VMEM((SLOTS, COLS, COLS), bf16),
            pltpu.VMEM((TILES, BLOCK, HALF), bf16),
            [pltpu.VMEM((PAIRS, BLOCK, HALF), bf16)] * 16,
            [pltpu.VMEM((NX - 1, SLOTS, BLOCK, HALF), bf16)] * 16,
            pltpu.VMEM((SLOTS, NZ, ROWS, HALF), bf16),
            pltpu.VMEM((ROWS, COLS), f32),
            pltpu.VMEM((ROWS, COLS), f32),
            pltpu.VMEM((ROWS, COLS), bf16),
            pltpu.VMEM((NO * PAD, ROWS), bf16),
            pltpu.VMEM((NO, PAD, COLS), bf16),
            pltpu.VMEM((NO - 1, PAD, COLS), bf16),
            pltpu.SMEM((TILES,), jnp.int32),
            pltpu.SMEM((TILES + 1,), jnp.int32),
            pltpu.SMEM((PAIRS,), jnp.int32),
            pltpu.SMEM((NX * SLOTS,), jnp.int32),
            dma, dma, dma, dma, dma, dma,
            dma((16,)), dma((16,)), dma((16,)), dma((16,)),
            dma, dma,
        ],
        compiler_params=pltpu.CompilerParams(
            collective_id=0, has_side_effects=True, vmem_limit_bytes=48 * 1024 * 1024
        ),
        name="sigma",
    )(
        triple_amps, double_amps, ladder_block_table, source_ids, list_length, partner, virtual_energy,
        triple_occupied_energy.reshape(1, ROWS), coupling, projector,
    )


def solution(mesh):
    return jax.shard_map(
        on_device,
        mesh=mesh,
        in_specs=(
            P("vir", "occ", None),
            P("vir", None, None),
            P("vir", None, None, None),
            P(),
            P(),
            P(),
            P("vir", None),
            P("occ"),
            P("occ", None),
            P("occ", None),
        ),
        out_specs=(P("vir", "occ", None), P("vir", "occ", None)),
        check_vma=False,
    )
```

```python
import jax
import jax.numpy as jnp
from jax import lax
from jax.experimental import pallas as pl
from jax.experimental.pallas import tpu as pltpu
from jax.sharding import PartitionSpec as P

MESH = pl.DeviceIdType.MESH

NX, NZ, NY, NO = 4, 2, 8, 8
TILES = NX * NZ * NY
PAIRS = TILES // 2
SLOTS = 6
ROWS = 512
COLS = 512
BLOCK = ROWS // (NX * NY)
HALF = COLS // NZ
OCCJ = 96
SHARE = OCCJ // NO
PAD = 16
OFFSETS = (0, -1, 1, -2, 2, -3, 3, 4)
NEAR = 7 * NX * BLOCK
QUOTA = PAIRS // 2


def kernel(
    t_hbm, da_hbm, ladder_hbm, ids_hbm, len_hbm, partner_hbm, ven_hbm, occ_hbm, coup_hbm, proj_hbm,
    out_ref, out2_ref,
    t_ref, da_ref, ids_ref, len_ref, partner_ref, ven_ref, occ_ref, coup_ref, proj_ref,
    ladder, chunks, ring, picked, sources, acc, base, low, proj_t, part, got,
    rank, following, first, pick,
    load_sem, p1_send, p1_recv, own_sem, z_send, z_recv, y_send, y_recv, x_send, x_recv, o_send, o_recv,
):
    vir, occ = lax.axis_index("vir"), lax.axis_index("occ")
    x, zh, y = vir // (NZ * NY), (vir // NY) % NZ, vir % NY

    def vir_at(dx, dz, dy):
        return ((x + dx) % NX) * (NZ * NY) + ((zh + dz) % NZ) * NY + (y + dy) % NY

    loads = [
        pltpu.make_async_copy(src, dst, load_sem.at[i])
        for i, (src, dst) in enumerate((
            (partner_hbm, partner_ref), (ids_hbm, ids_ref), (len_hbm, len_ref), (occ_hbm, occ_ref),
            (proj_hbm, proj_ref), (coup_hbm, coup_ref), (da_hbm.at[0], da_ref), (ven_hbm, ven_ref),
            (t_hbm.at[0], t_ref), (ladder_hbm.at[0], ladder),
        ))
    ]
    for load in loads:
        load.start()

    barrier = pltpu.get_barrier_semaphore()

    def for_others(act):
        for dx in range(NX):
            for dz in range(NZ):
                place = lax.rem(x + dx, NX) * (NZ * NY) + lax.rem(zh + dz, NZ) * NY

                @pl.loop(0 if dx + dz else 1, NY)
                def _(dy, place=place):
                    act(place + lax.rem(y + dy, NY))

    def greet(v):
        pl.semaphore_signal(barrier, inc=1, device_id=(v, occ), device_id_type=MESH)

    for_others(greet)

    @pl.loop(1, NO)
    def _(j):
        pl.semaphore_signal(barrier, inc=1, device_id=(vir, lax.rem(occ + j, NO)), device_id_type=MESH)

    for load in loads[:3]:
        load.wait()

    @pl.loop(0, TILES)
    def _(t):
        rank[t] = 0

    def number(t, count):
        other = partner_ref[t]
        lower = t < other
        rank[t] = jnp.where(lower, count, rank[other])
        return count + lower.astype(jnp.int32)

    lax.fori_loop(0, TILES, number, jnp.int32(0))
    following[TILES] = 0

    def look_back(i, nxt):
        t = TILES - 1 - i
        nxt = jnp.where(t < partner_ref[t], t, nxt)
        following[t] = nxt
        return nxt

    lax.fori_loop(0, TILES, look_back, jnp.int32(0))

    def list_first(k, t):
        low_tile = following[t]
        first[k] = low_tile
        return low_tile + 1

    lax.fori_loop(0, PAIRS, list_first, jnp.int32(0))

    for j in range(NX):
        for l in range(SLOTS):
            pick[j * SLOTS + l] = rank[ids_ref[l, vir_at(j, 0, 0)]]

    pl.semaphore_wait(barrier, TILES + NO - 2)

    def chunk_of(v):
        vx, vz, vy = v // (NZ * NY), (v // NY) % NZ, v % NY
        return t_hbm.at[
            0,
            pl.ds(pl.multiple_of(vx * (NY * BLOCK) + vy * BLOCK, BLOCK), BLOCK),
            pl.ds(pl.multiple_of(vz * HALF, HALF), HALF),
        ]

    def spread(v):
        pltpu.make_async_remote_copy(
            src_ref=chunk_of(v), dst_ref=chunks.at[vir], send_sem=p1_send, recv_sem=p1_recv,
            device_id=(v, occ), device_id_type=MESH,
        ).start()

    for_others(spread)

    keep = pltpu.make_async_copy(chunk_of(vir), chunks.at[vir], own_sem)
    keep.start()

    keep.wait()
    arrived = chunks.at[0 : TILES - 1]
    pltpu.make_async_copy(arrived, arrived, p1_recv).wait()

    def differences(q):
        @pl.loop(q * QUOTA, (q + 1) * QUOTA)
        def _(k):
            tile = first[k]
            ring[0][k] = (
                chunks[tile].astype(jnp.float32) - chunks[partner_ref[tile]].astype(jnp.float32)
            ).astype(jnp.bfloat16)

    sent = []

    def send(src, dst, send_sem, recv_sem, to):
        copy = pltpu.make_async_remote_copy(
            src_ref=src, dst_ref=dst, send_sem=send_sem, recv_sem=recv_sem, device_id=to, device_id_type=MESH
        )
        copy.start()
        return copy

    def arrival(dst, sem):
        pltpu.make_async_copy(dst, dst, sem).wait()

    up, down = (vir_at(0, 0, 1), occ), (vir_at(0, 0, -1), occ)

    def at_place(h, way, step):
        return ring[h * 8 + (0 if step == 0 else 7 if step == 4 else 2 * step - 1 + way)]

    def ways(step, q):
        return (q,) if step == 4 else (0, 1)

    def pass_on(h, step, q):
        part_q = slice(q * QUOTA, (q + 1) * QUOTA)
        for way in ways(step + 1, q):
            i = ((h * 4 + step) * 2 + way) * 2 + q
            sent.append(
                send(
                    at_place(h, way, step).at[part_q], at_place(h, way, step + 1).at[part_q],
                    y_send.at[i], y_recv.at[i], (up, down)[way],
                )
            )

    def await_step(h, step, q):
        part_q = slice(q * QUOTA, (q + 1) * QUOTA)
        if step == 0:
            arrival(ring[h * 8].at[part_q], z_recv.at[q])
            return
        for way in ways(step, q):
            arrival(at_place(h, way, step).at[part_q], y_recv.at[((h * 4 + step - 1) * 2 + way) * 2 + q])

    def deal(h, s):
        block, out = ring[h * 8 + s], picked[h * 8 + s]
        half = zh if h == 0 else 1 - zh
        where = pl.ds(pl.multiple_of(s * NX * BLOCK + x * BLOCK, BLOCK), BLOCK)
        for j in range(1, NX):
            for l in range(SLOTS):
                out[j - 1, l] = block[pick[j * SLOTS + l]]
            send(
                out.at[j - 1], sources.at[:, half, where, :], x_send.at[h * 8 + s], x_recv.at[h * 8 + s],
                (vir_at(j, 0, 0), occ),
            )
        for l in range(SLOTS):
            sources[l, half, where, :] = block[pick[l]]

    def deal_step(h, step):
        if step == 0:
            deal(h, 0)
        elif step == 4:
            deal(h, 7)
        else:
            deal(h, 2 * step - 1)
            deal(h, 2 * step)

    for q in range(2):
        differences(q)
        part_q = slice(q * QUOTA, (q + 1) * QUOTA)
        pass_on(0, 0, q)
        sent.append(
            send(ring[0].at[part_q], ring[8].at[part_q], z_send.at[q], z_recv.at[q], (vir_at(0, 1, 0), occ))
        )
    deal_step(0, 0)

    for load in loads[3:9]:
        load.wait()
    proj_t[...] = jnp.zeros_like(proj_t)
    for o in range(NO):
        proj_t[PAD * o : PAD * o + SHARE, :] = proj_ref[SHARE * o : SHARE * (o + 1), :]
    for i in range(ROWS // 128):
        rows = slice(128 * i, 128 * (i + 1))
        column = jnp.broadcast_to(occ_ref[:, rows], (128, 128)).T
        wide = jnp.concatenate([column] * (COLS // 128), axis=1)
        couple = lax.dot_general(
            coup_ref[:, rows], da_ref[...], (((0,), (0,)), ((), ())), preferred_element_type=jnp.float32
        )
        base[rows, :] = couple + (ven_ref[...] - wide) * t_ref[rows, :].astype(jnp.float32)

    loads[9].wait()
    for l in range(SLOTS):
        tile = ids_ref[l, vir]
        sign = jnp.where(tile < partner_ref[tile], 1.0, -1.0)
        factor = jnp.where(l < len_ref[vir], sign, 0.0).astype(jnp.float32)
        ladder[l] = (ladder[l].astype(jnp.float32) * factor).astype(jnp.bfloat16)

    for h, step in ((0, 1), (0, 2), (1, 0), (0, 3), (1, 1), (0, 4), (1, 2), (1, 3), (1, 4)):
        for q in range(2):
            await_step(h, step, q)
            if step < 4:
                pass_on(h, step, q)
        deal_step(h, step)

    def multiply(begin, end):
        for s in range(8):
            if begin <= s * NX * BLOCK < end:
                for h in range(2):
                    arrival(picked[h * 8 + s], x_recv.at[h * 8 + s])
        acc[begin:end] = jnp.zeros((end - begin, COLS), jnp.float32)

        @pl.loop(0, SLOTS)
        def _(l):
            acc[begin:end] += jnp.dot(
                sources[l, 0, begin:end, :], ladder[l, 0:HALF, :], preferred_element_type=jnp.float32
            ) + jnp.dot(sources[l, 1, begin:end, :], ladder[l, HALF:COLS, :], preferred_element_type=jnp.float32)

        @pl.loop(begin // BLOCK, end // BLOCK)
        def _(b):
            s, bx = b // NX, b % NX
            offset = (s // 2) * (1 - s % 2) - ((s + 1) // 2) * (s % 2)
            rows = pl.ds(pl.multiple_of(bx * (NY * BLOCK) + ((y + offset + NY) % NY) * BLOCK, BLOCK), BLOCK)
            total = base[rows, :] + acc[pl.ds(pl.multiple_of(b * BLOCK, BLOCK), BLOCK), :]
            high = total.astype(jnp.bfloat16)
            out_ref[0, rows, :] = high
            low[rows, :] = (total - high.astype(jnp.float32)).astype(jnp.bfloat16)

    multiply(0, NEAR)
    multiply(NEAR, ROWS)

    both = jnp.dot(proj_t[...], out_ref[0], preferred_element_type=jnp.float32) + jnp.dot(
        proj_t[...], low[...], preferred_element_type=jnp.float32
    )
    for o in range(NO):
        part[o] = both[PAD * o : PAD * (o + 1), :].astype(jnp.bfloat16)

    @pl.loop(1, NO)
    def _(j):
        to = (occ + j) % NO
        send(part.at[to], got.at[j - 1], o_send, o_recv, (vir, to))

    arrival(got, o_recv)
    total = part[occ].astype(jnp.float32)
    for j in range(NO - 1):
        total = total + got[j].astype(jnp.float32)
    out2_ref[:, 0, :] = total[0:SHARE, :]

    for copy in sent:
        copy.wait_send()
    pltpu.make_async_copy(arrived, arrived, p1_send).wait()
    for i in range(16):
        pltpu.make_async_copy(picked[i], picked[i], x_send.at[i]).wait()
    pltpu.make_async_copy(got, got, o_send).wait()


def on_device(
    triple_amps, double_amps, ladder_block_table, source_ids, list_length, partner, virtual_energy,
    triple_occupied_energy, coupling, projector,
):
    vmem, hbm = pl.BlockSpec(memory_space=pltpu.VMEM), pl.BlockSpec(memory_space=pltpu.HBM)
    bf16, f32, i32 = jnp.bfloat16, jnp.float32, jnp.int32
    dma = pltpu.SemaphoreType.DMA
    arrays = (
        triple_amps, double_amps, ladder_block_table, source_ids.T, list_length, partner, virtual_energy,
        triple_occupied_energy.reshape(1, ROWS), coupling.T, projector.T,
    )
    sigma_triples, sigma_doubles = pl.pallas_call(
        kernel,
        out_shape=(
            jax.ShapeDtypeStruct((1, ROWS, COLS), bf16),
            jax.ShapeDtypeStruct((SHARE, 1, COLS), f32),
        ),
        in_specs=[hbm] * len(arrays),
        out_specs=(vmem, vmem),
        scratch_shapes=[
            pltpu.VMEM((ROWS, COLS), bf16),
            pltpu.VMEM((OCCJ, COLS), bf16),
            pltpu.SMEM((SLOTS, TILES), i32),
            pltpu.SMEM((TILES,), i32),
            pltpu.SMEM((TILES,), i32),
            pltpu.VMEM((1, COLS), f32),
            pltpu.VMEM((1, ROWS), f32),
            pltpu.VMEM((OCCJ, ROWS), bf16),
            pltpu.VMEM((OCCJ, ROWS), bf16),
            pltpu.VMEM((SLOTS, COLS, COLS), bf16),
            pltpu.VMEM((TILES, BLOCK, HALF), bf16),
            [pltpu.VMEM((PAIRS, BLOCK, HALF), bf16)] * 16,
            [pltpu.VMEM((NX - 1, SLOTS, BLOCK, HALF), bf16)] * 16,
            pltpu.VMEM((SLOTS, NZ, ROWS, HALF), bf16),
            pltpu.VMEM((ROWS, COLS), f32),
            pltpu.VMEM((ROWS, COLS), f32),
            pltpu.VMEM((ROWS, COLS), bf16),
            pltpu.VMEM((NO * PAD, ROWS), bf16),
            pltpu.VMEM((NO, PAD, COLS), bf16),
            pltpu.VMEM((NO - 1, PAD, COLS), bf16),
            pltpu.SMEM((TILES,), jnp.int32),
            pltpu.SMEM((TILES + 1,), jnp.int32),
            pltpu.SMEM((PAIRS,), jnp.int32),
            pltpu.SMEM((NX * SLOTS,), jnp.int32),
            dma((10,)), dma, dma, dma, dma((2,)), dma((2,)),
            dma((32,)), dma((32,)), dma((16,)), dma((16,)),
            dma, dma,
        ],
        compiler_params=pltpu.CompilerParams(
            collective_id=0, has_side_effects=True, vmem_limit_bytes=48 * 1024 * 1024
        ),
        name="sigma",
    )(*(pltpu.with_memory_space_constraint(a, pltpu.HBM) for a in arrays))
    return sigma_triples, jnp.swapaxes(sigma_doubles, 0, 1)


def solution(mesh):
    return jax.shard_map(
        on_device,
        mesh=mesh,
        in_specs=(
            P("vir", "occ", None),
            P("vir", None, None),
            P("vir", None, None, None),
            P(),
            P(),
            P(),
            P("vir", None),
            P("occ"),
            P("occ", None),
            P("occ", None),
        ),
        out_specs=(P("vir", "occ", None), P("vir", "occ", None)),
        check_vma=False,
    )
```

```python
import jax
import jax.numpy as jnp
from jax import lax
from jax.experimental import pallas as pl
from jax.experimental.pallas import tpu as pltpu
from jax.sharding import PartitionSpec as P

MESH = pl.DeviceIdType.MESH

NX, NZ, NY, NO = 4, 2, 8, 8
TILES = NX * NZ * NY
PAIRS = TILES // 2
SLOTS = 6
ROWS = 512
COLS = 512
BLOCK = ROWS // (NX * NY)
HALF = COLS // NZ
OCCJ = 96
SHARE = OCCJ // NO
PAD = 16
QUARTER = HALF // 2
OFFSETS = (0, -1, 1, -2, 2, -3, 3, 4)
PLACE = NX * BLOCK
NEAR = 5 * PLACE
LAST = 3 * PLACE
THIRD = SLOTS // 2
FOLD = 384


def kernel(
    t_hbm, da_hbm, ladder_hbm, ids_hbm, len_hbm, partner_hbm, ven_hbm, occ_hbm, coup_hbm, proj_hbm,
    out_ref, out2_ref,
    t_ref, da_ref, ids_ref, len_ref, partner_ref, ven_ref, occ_ref, coup_ref, proj_ref,
    ladder, chunks, ring, picked, far, sources, acc, base, low, last, near, proj_t, proj_last, part, got,
    rank, following, first, pick,
    ready, ready_occ, ready_all, load_sem, p1_send, p1_recv, own_sem, z_send, z_recv, y_send, y_recv, x_send, x_recv, far_send, o_send, o_recv,
):
    vir, occ = lax.axis_index("vir"), lax.axis_index("occ")
    x, zh, y = vir // (NZ * NY), (vir // NY) % NZ, vir % NY

    def vir_at(dx, dz, dy):
        return ((x + dx) % NX) * (NZ * NY) + ((zh + dz) % NZ) * NY + (y + dy) % NY

    loads = [
        pltpu.make_async_copy(src, dst, load_sem.at[i])
        for i, (src, dst) in enumerate((
            (partner_hbm, partner_ref), (ids_hbm, ids_ref), (len_hbm, len_ref), (occ_hbm, occ_ref),
            (proj_hbm, proj_ref), (coup_hbm, coup_ref), (da_hbm.at[0], da_ref), (ven_hbm, ven_ref),
            (t_hbm.at[0], t_ref), (ladder_hbm.at[0], ladder),
        ))
    ]

    barrier = pltpu.get_barrier_semaphore()

    def for_plane(dz, act):
        for dx in range(NX):
            place = lax.rem(x + dx, NX) * (NZ * NY) + lax.rem(zh + dz, NZ) * NY

            @pl.loop(0 if dx + dz else 1, NY)
            def _(dy, place=place):
                act(place + lax.rem(y + dy, NY))

    def for_occ(act):
        @pl.loop(1, NO)
        def _(j):
            act((vir, lax.rem(occ + j, NO)))

    def greet(to, sem):
        pl.semaphore_signal(sem, inc=1, device_id=to, device_id_type=MESH)

    def chunk_of(v, q):
        vx, vz, vy = v // (NZ * NY), (v // NY) % NZ, v % NY
        return t_hbm.at[
            0,
            pl.ds(pl.multiple_of(vx * (NY * BLOCK) + vy * BLOCK, BLOCK), BLOCK),
            pl.ds(pl.multiple_of(vz * HALF + q * QUARTER, QUARTER), QUARTER),
        ]

    def spread(dz, q):
        def to(v):
            pltpu.make_async_remote_copy(
                src_ref=chunk_of(v, q), dst_ref=chunks[q].at[vir], send_sem=p1_send.at[q], recv_sem=p1_recv.at[q],
                device_id=(v, occ), device_id_type=MESH,
            ).start()

        for_plane(dz, to)

    def number_pairs():
        for load in loads[:3]:
            load.wait()

        @pl.loop(0, TILES)
        def _(t):
            rank[t] = 0

        def number(t, count):
            other = partner_ref[t]
            lower = t < other
            rank[t] = jnp.where(lower, count, rank[other])
            return count + lower.astype(jnp.int32)

        lax.fori_loop(0, TILES, number, jnp.int32(0))
        following[TILES] = 0

        def look_back(i, nxt):
            t = TILES - 1 - i
            nxt = jnp.where(t < partner_ref[t], t, nxt)
            following[t] = nxt
            return nxt

        lax.fori_loop(0, TILES, look_back, jnp.int32(0))

        def list_first(k, t):
            low_tile = following[t]
            first[k] = low_tile
            return low_tile + 1

        lax.fori_loop(0, PAIRS, list_first, jnp.int32(0))

        for j in range(NX):
            for l in range(SLOTS):
                pick[j * SLOTS + l] = rank[ids_ref[l, vir_at(j, 0, 0)]]
            for way in range(2):
                for i in range(THIRD):
                    pick[NX * SLOTS + (way * NX + j) * THIRD + i] = rank[
                        ids_ref[way * THIRD + i, vir_at(j, 0, 1 - 2 * way)]
                    ]

    plane = NX * NY
    partner_plane = (vir_at(0, 1, 0), occ)

    @pl.when(zh == 0)
    def _():
        for_plane(0, lambda v: greet((v, occ), barrier))
        for_occ(lambda to: greet(to, barrier))
        for load in loads:
            load.start()
        pl.semaphore_wait(barrier, plane - 1 + NO - 1)
        for_plane(1, lambda v: greet((v, occ), barrier))
        for q in range(2):
            spread(0, q)
        number_pairs()
        pl.semaphore_wait(barrier, plane)
        greet(partner_plane, ready)
        for q in range(2):
            spread(1, q)
        for_occ(lambda to: greet(to, ready_occ))

    @pl.when(zh == 1)
    def _():
        pl.semaphore_wait(barrier, plane)
        for_plane(1, lambda v: greet((v, occ), barrier))
        for load in loads:
            load.start()
        for q in range(2):
            spread(1, q)
        number_pairs()
        pl.semaphore_wait(ready, 1)
        for q in range(2):
            spread(0, q)

    kept = [pltpu.make_async_copy(chunk_of(vir, q), chunks[q].at[vir], own_sem.at[q]) for q in range(2)]
    for keep in kept:
        keep.start()

    def differences(q):
        kept[q].wait()
        arrived = chunks[q].at[0 : TILES - 1]
        pltpu.make_async_copy(arrived, arrived, p1_recv.at[q]).wait()

        @pl.loop(0, PAIRS)
        def _(k):
            tile = first[k]
            ring[q][k] = (
                chunks[q][tile].astype(jnp.float32) - chunks[q][partner_ref[tile]].astype(jnp.float32)
            ).astype(jnp.bfloat16)

    sent = []

    def send(src, dst, send_sem, recv_sem, to):
        copy = pltpu.make_async_remote_copy(
            src_ref=src, dst_ref=dst, send_sem=send_sem, recv_sem=recv_sem, device_id=to, device_id_type=MESH
        )
        copy.start()
        return copy

    def arrival(dst, sem):
        pltpu.make_async_copy(dst, dst, sem).wait()

    up, down = (vir_at(0, 0, 1), occ), (vir_at(0, 0, -1), occ)

    def at_place(h, way, step, q):
        return ring[(h * 7 + (0 if step == 0 else 2 * step - 1 + way)) * 2 + q]

    def pass_on(h, step, q):
        for way in range(2):
            i = ((h * 3 + step) * 2 + way) * 2 + q
            sent.append(
                send(
                    at_place(h, way, step, q), at_place(h, way, step + 1, q),
                    y_send.at[i], y_recv.at[i], (up, down)[way],
                )
            )

    def await_step(h, step, q):
        if step == 0:
            arrival(at_place(h, 0, 0, q), z_recv.at[q])
            return
        for way in range(2):
            arrival(at_place(h, way, step, q), y_recv.at[((h * 3 + step - 1) * 2 + way) * 2 + q])

    def target(slots, h, s, q):
        rows = pl.ds(pl.multiple_of(s * PLACE + x * BLOCK, BLOCK), BLOCK)
        return sources.at[slots, zh if h == 0 else 1 - zh, rows, q * QUARTER : (q + 1) * QUARTER]

    def deal(h, s, q):
        i = (h * 7 + s) * 2 + q
        block, out = ring[i], picked[i]
        for j in range(1, NX):
            for l in range(SLOTS):
                out[j - 1, l] = block[pick[j * SLOTS + l]]
            send(
                out.at[j - 1], target(slice(0, SLOTS), h, s, q), x_send.at[i], x_recv.at[(h * 8 + s) * 2 + q],
                (vir_at(j, 0, 0), occ),
            )
        for l in range(SLOTS):
            target(l, h, s, q)[...] = block[pick[l]]

    def deal_far(h, way, q):
        block, out = ring[(h * 7 + 5 + way) * 2 + q], far[h * 2 + q]
        for j in range(NX):
            for i in range(THIRD):
                out[way, j, i] = block[pick[NX * SLOTS + (way * NX + j) * THIRD + i]]
            send(
                out.at[way, j], target(slice(way * THIRD, (way + 1) * THIRD), h, 7, q),
                far_send.at[(h * 2 + way) * 2 + q], x_recv.at[(h * 8 + 7) * 2 + q], (vir_at(j, 0, 1 - 2 * way), occ),
            )

    def deal_step(h, step, q):
        if step == 3:
            deal_far(h, 0, q)
            deal_far(h, 1, q)
        if step == 0:
            deal(h, 0, q)
        else:
            deal(h, 2 * step - 1, q)
            deal(h, 2 * step, q)

    def prepare_projector():
        proj_t[...] = jnp.zeros_like(proj_t)
        for o in range(NO):
            proj_t[PAD * o : PAD * o + SHARE, :] = proj_ref[SHARE * o : SHARE * (o + 1), :]
        row = lax.broadcasted_iota(jnp.int32, (ROWS, LAST), 0)
        column = lax.broadcasted_iota(jnp.int32, (ROWS, LAST), 1)
        into = jnp.zeros((ROWS, LAST), jnp.int32)
        for i in range(LAST // BLOCK):
            b = NEAR // BLOCK + i
            into = jnp.where((column >= i * BLOCK) & (column < (i + 1) * BLOCK), row_of(b) - i * BLOCK, into)
        chosen = (row == column + into).astype(jnp.bfloat16)
        proj_last[...] = jnp.dot(proj_t[...], chosen, preferred_element_type=jnp.float32).astype(jnp.bfloat16)
        for i in range(LAST // BLOCK):
            rows = pl.ds(row_of(NEAR // BLOCK + i), BLOCK)
            out_ref[0, rows, :] = jnp.zeros((BLOCK, COLS), jnp.bfloat16)
            low[rows, :] = jnp.zeros((BLOCK, COLS), jnp.bfloat16)

    def prepare_base(i):
        rows = slice(128 * i, 128 * (i + 1))
        column = jnp.broadcast_to(occ_ref[:, rows], (128, 128)).T
        wide = jnp.concatenate([column] * (COLS // 128), axis=1)
        couple = lax.dot_general(
            coup_ref[:, rows], da_ref[...], (((0,), (0,)), ((), ())), preferred_element_type=jnp.float32
        )
        base[rows, :] = couple + (ven_ref[...] - wide) * t_ref[rows, :].astype(jnp.float32)

    def prepare_ladder(l):
        tile = ids_ref[l, vir]
        sign = jnp.where(tile < partner_ref[tile], 1.0, -1.0)
        factor = jnp.where(l < len_ref[vir], sign, 0.0).astype(jnp.float32)
        ladder[l] = (ladder[l].astype(jnp.float32) * factor).astype(jnp.bfloat16)

    def row_of(b):
        s, bx = b // NX, b % NX
        offset = (s // 2) * (1 - s % 2) - ((s + 1) // 2) * (s % 2)
        return pl.multiple_of(bx * (NY * BLOCK) + lax.rem(y + offset + NY, NY) * BLOCK, BLOCK)

    for q in range(2):
        differences(q)
        pass_on(0, 0, q)
        sent.append(send(ring[q], ring[14 + q], z_send.at[q], z_recv.at[q], (vir_at(0, 1, 0), occ)))
    for q in range(2):
        deal_step(0, 0, q)
    @pl.when(zh == 0)
    def _():
        pl.semaphore_wait(ready_occ, NO - 1)
        greet(partner_plane, ready_all)

    for load in loads[3:]:
        load.wait()

    for h, step in ((0, 1), (0, 2), (0, 3), (1, 0), (1, 1), (1, 2), (1, 3)):
        for q in range(2):
            await_step(h, step, q)
            if step < 3:
                pass_on(h, step, q)
            if step == 3:
                deal_step(h, step, q)
        if step < 3:
            for q in range(2):
                deal_step(h, step, q)
        if (h, step) == (0, 1):
            prepare_projector()
        elif (h, step) == (0, 2):
            for i in range(2):
                prepare_base(i)
        elif (h, step) == (0, 3):
            for i in range(2, 4):
                prepare_base(i)
        elif (h, step) == (1, 0):
            for l in range(3):
                prepare_ladder(l)
        elif (h, step) == (1, 1):
            for l in range(3, 6):
                prepare_ladder(l)

    def multiply(begin, end):
        for s in range(begin // PLACE, end // PLACE):
            for i in range(4):
                h, q = i // 2, i % 2
                arrival(picked[(h * 7 + s) * 2 + q] if s < 7 else far[i], x_recv.at[(h * 8 + s) * 2 + q])
        acc[begin:end] = jnp.zeros((end - begin, COLS), jnp.float32)

        @pl.loop(0, SLOTS)
        def _(l):
            acc[begin:end] += jnp.dot(
                sources[l, 0, begin:end, :], ladder[l, 0:HALF, :], preferred_element_type=jnp.float32
            ) + jnp.dot(sources[l, 1, begin:end, :], ladder[l, HALF:COLS, :], preferred_element_type=jnp.float32)

    def finish(b):
        rows = pl.ds(row_of(b), BLOCK)
        total = base[rows, :] + acc[pl.ds(pl.multiple_of(b * BLOCK, BLOCK), BLOCK), :]
        high = total.astype(jnp.bfloat16)
        out_ref[0, rows, :] = high
        return rows, high, (total - high.astype(jnp.float32)).astype(jnp.bfloat16)

    multiply(0, NEAR)

    @pl.loop(0, NEAR // BLOCK)
    def _(b):
        rows, _, rest = finish(b)
        low[rows, :] = rest

    near[...] = jnp.dot(proj_t[...], out_ref[0], preferred_element_type=jnp.float32) + jnp.dot(
        proj_t[...], low[...], preferred_element_type=jnp.float32
    )
    multiply(NEAR, ROWS)

    @pl.loop(0, LAST // BLOCK)
    def _(i):
        _, high, rest = finish(NEAR // BLOCK + i)
        rows = pl.ds(pl.multiple_of(i * BLOCK, BLOCK), BLOCK)
        last[0, rows, :] = high
        last[1, rows, :] = rest

    both = (
        near[...]
        + jnp.dot(proj_last[...], last[0], preferred_element_type=jnp.float32)
        + jnp.dot(proj_last[...], last[1], preferred_element_type=jnp.float32)
    )
    for o in range(NO):
        mine = both[PAD * o : PAD * (o + 1), :]
        rest = [mine[4 * m : 4 * (m + 1), FOLD:] for m in range(3)]
        part[o] = jnp.concatenate(
            [mine[0:SHARE, 0:FOLD], jnp.concatenate(rest, axis=1)], axis=0
        ).astype(jnp.bfloat16)

    @pl.when(zh == 1)
    def _():
        pl.semaphore_wait(ready_all, 1)

    @pl.loop(1, NO)
    def _(j):
        to = lax.rem(occ + j, NO)
        send(part.at[to], got.at[j - 1], o_send, o_recv, (vir, to))

    arrival(got, o_recv)
    total = part[occ].astype(jnp.float32)
    for j in range(NO - 1):
        total = total + got[j].astype(jnp.float32)
    out2_ref[:, 0, 0:FOLD] = total[0:SHARE, :]
    for m in range(3):
        out2_ref[4 * m : 4 * (m + 1), 0, FOLD:] = total[SHARE:, 128 * m : 128 * (m + 1)]

    for copy in sent:
        copy.wait_send()
    for q in range(2):
        arrived = chunks[q].at[0 : TILES - 1]
        pltpu.make_async_copy(arrived, arrived, p1_send.at[q]).wait()
    for i in range(28):
        pltpu.make_async_copy(picked[i], picked[i], x_send.at[i]).wait()
    for i in range(8):
        h, way, q = i // 4, (i // 2) % 2, i % 2
        dealt = far[h * 2 + q].at[way]
        pltpu.make_async_copy(dealt, dealt, far_send.at[i]).wait()
    pltpu.make_async_copy(got, got, o_send).wait()


def on_device(
    triple_amps, double_amps, ladder_block_table, source_ids, list_length, partner, virtual_energy,
    triple_occupied_energy, coupling, projector,
):
    vmem, hbm = pl.BlockSpec(memory_space=pltpu.VMEM), pl.BlockSpec(memory_space=pltpu.HBM)
    bf16, f32, i32 = jnp.bfloat16, jnp.float32, jnp.int32
    dma = pltpu.SemaphoreType.DMA
    arrays = (
        triple_amps, double_amps, ladder_block_table, source_ids.T, list_length, partner, virtual_energy,
        triple_occupied_energy.reshape(1, ROWS), coupling.T, projector.T,
    )
    sigma_triples, sigma_doubles = pl.pallas_call(
        kernel,
        out_shape=(
            jax.ShapeDtypeStruct((1, ROWS, COLS), bf16),
            jax.ShapeDtypeStruct((SHARE, 1, COLS), f32),
        ),
        in_specs=[hbm] * len(arrays),
        out_specs=(vmem, vmem),
        scratch_shapes=[
            pltpu.VMEM((ROWS, COLS), bf16),
            pltpu.VMEM((OCCJ, COLS), bf16),
            pltpu.SMEM((SLOTS, TILES), i32),
            pltpu.SMEM((TILES,), i32),
            pltpu.SMEM((TILES,), i32),
            pltpu.VMEM((1, COLS), f32),
            pltpu.VMEM((1, ROWS), f32),
            pltpu.VMEM((OCCJ, ROWS), bf16),
            pltpu.VMEM((OCCJ, ROWS), bf16),
            pltpu.VMEM((SLOTS, COLS, COLS), bf16),
            [pltpu.VMEM((TILES, BLOCK, QUARTER), bf16)] * 2,
            [pltpu.VMEM((PAIRS, BLOCK, QUARTER), bf16)] * 28,
            [pltpu.VMEM((NX - 1, SLOTS, BLOCK, QUARTER), bf16)] * 28,
            [pltpu.VMEM((2, NX, THIRD, BLOCK, QUARTER), bf16)] * 4,
            pltpu.VMEM((SLOTS, NZ, ROWS, HALF), bf16),
            pltpu.VMEM((ROWS, COLS), f32),
            pltpu.VMEM((ROWS, COLS), f32),
            pltpu.VMEM((ROWS, COLS), bf16),
            pltpu.VMEM((2, LAST, COLS), bf16),
            pltpu.VMEM((NO * PAD, COLS), f32),
            pltpu.VMEM((NO * PAD, ROWS), bf16),
            pltpu.VMEM((NO * PAD, LAST), bf16),
            pltpu.VMEM((NO, PAD, FOLD), bf16),
            pltpu.VMEM((NO - 1, PAD, FOLD), bf16),
            pltpu.SMEM((TILES,), jnp.int32),
            pltpu.SMEM((TILES + 1,), jnp.int32),
            pltpu.SMEM((PAIRS,), jnp.int32),
            pltpu.SMEM((2 * NX * SLOTS,), jnp.int32),
            pltpu.SemaphoreType.REGULAR, pltpu.SemaphoreType.REGULAR, pltpu.SemaphoreType.REGULAR,
            dma((10,)), dma((2,)), dma((2,)), dma((2,)), dma((2,)), dma((2,)),
            dma((24,)), dma((24,)), dma((28,)), dma((32,)), dma((8,)),
            dma, dma,
        ],
        compiler_params=pltpu.CompilerParams(
            collective_id=0, has_side_effects=True, vmem_limit_bytes=48 * 1024 * 1024
        ),
        name="sigma",
    )(*(pltpu.with_memory_space_constraint(a, pltpu.HBM) for a in arrays))
    return sigma_triples, jnp.swapaxes(sigma_doubles, 0, 1)


def solution(mesh):
    return jax.shard_map(
        on_device,
        mesh=mesh,
        in_specs=(
            P("vir", "occ", None),
            P("vir", None, None),
            P("vir", None, None, None),
            P(),
            P(),
            P(),
            P("vir", None),
            P("occ"),
            P("occ", None),
            P("occ", None),
        ),
        out_specs=(P("vir", "occ", None), P("vir", "occ", None)),
        check_vma=False,
    )
```

```python
import jax
import jax.numpy as jnp
from jax import lax
from jax.experimental import pallas as pl
from jax.experimental.pallas import tpu as pltpu
from jax.sharding import PartitionSpec as P

MESH = pl.DeviceIdType.MESH

NX, NZ, NY, NO = 4, 2, 8, 8
TILES = NX * NZ * NY
PAIRS = TILES // 2
SLOTS = 6
ROWS = 512
COLS = 512
BLOCK = ROWS // (NX * NY)
HALF = COLS // NZ
OCCJ = 96
SHARE = OCCJ // NO
PAD = 16
QUARTER = HALF // 2
OFFSETS = (0, -1, 1, -2, 2, -3, 3, 4)
PLACE = NX * BLOCK
EARLY = 3 * PLACE
NEAR = 5 * PLACE
LAST = 3 * PLACE
THIRD = SLOTS // 2
FOLD = 384


def kernel(
    t_hbm, da_hbm, ladder_hbm, ids_hbm, len_hbm, partner_hbm, ven_hbm, occ_hbm, coup_hbm, proj_hbm,
    out_ref, out2_ref,
    t_ref, da_ref, ids_ref, len_ref, partner_ref, ven_ref, occ_ref, coup_ref, proj_ref,
    ladder, chunks, ring, picked, across, far, sources, weights, acc, base, low, last, near, proj_t, proj_last, part, got,
    rank, following, first, pick,
    load_sem, p1_send, p1_recv, own_sem, z_send, z_recv, y_send, y_recv, x_send, x_recv, far_send, o_send, o_recv,
):
    vir, occ = lax.axis_index("vir"), lax.axis_index("occ")
    x, zh, y = vir // (NZ * NY), (vir // NY) % NZ, vir % NY

    def vir_at(dx, dz, dy):
        return ((x + dx) % NX) * (NZ * NY) + ((zh + dz) % NZ) * NY + (y + dy) % NY

    barrier = pltpu.get_barrier_semaphore()

    def in_vir(vx, vz, vy):
        return (vx * (NZ * NY) + vz * NY + vy, occ)

    def for_others(act):
        for dx in range(NX):
            for dz in range(NZ):
                vx, vz = lax.rem(x + dx, NX), lax.rem(zh + dz, NZ)

                @pl.loop(0 if dx + dz else 1, NY)
                def _(dy, vx=vx, vz=vz):
                    act(vx, vz, lax.rem(y + dy, NY))

    def greet(*at):
        pl.semaphore_signal(barrier, inc=1, device_id=in_vir(*at), device_id_type=MESH)

    for_others(greet)

    @pl.loop(1, NO)
    def _(j):
        pl.semaphore_signal(barrier, inc=1, device_id=(vir, lax.rem(occ + j, NO)), device_id_type=MESH)

    loads = [
        pltpu.make_async_copy(src, dst, load_sem.at[i])
        for i, (src, dst) in enumerate((
            (partner_hbm, partner_ref), (ids_hbm, ids_ref), (len_hbm, len_ref), (occ_hbm, occ_ref),
            (proj_hbm, proj_ref), (coup_hbm, coup_ref), (da_hbm.at[0], da_ref), (ven_hbm, ven_ref),
            (t_hbm.at[0], t_ref), (ladder_hbm.at[0], ladder),
        ))
    ]
    for load in loads:
        load.start()

    pl.semaphore_wait(barrier, TILES + NO - 2)

    def chunk_of(vx, vz, vy, q):
        return t_hbm.at[
            0,
            pl.ds(pl.multiple_of(vx * (NY * BLOCK) + vy * BLOCK, BLOCK), BLOCK),
            pl.ds(pl.multiple_of(vz * HALF + q * QUARTER, QUARTER), QUARTER),
        ]

    def spread(q):
        def to(*at):
            pltpu.make_async_remote_copy(
                src_ref=chunk_of(*at, q), dst_ref=chunks[q].at[vir], send_sem=p1_send.at[q], recv_sem=p1_recv.at[q],
                device_id=in_vir(*at), device_id_type=MESH,
            ).start()

        for_others(to)
        keep = pltpu.make_async_copy(chunk_of(x, zh, y, q), chunks[q].at[vir], own_sem.at[q])
        keep.start()
        return keep

    kept = [spread(q) for q in range(2)]

    for load in loads[:3]:
        load.wait()

    @pl.loop(0, TILES)
    def _(t):
        rank[t] = 0

    def number(t, count):
        other = partner_ref[t]
        lower = t < other
        rank[t] = jnp.where(lower, count, rank[other])
        return count + lower.astype(jnp.int32)

    lax.fori_loop(0, TILES, number, jnp.int32(0))
    following[TILES] = 0

    def look_back(i, nxt):
        t = TILES - 1 - i
        nxt = jnp.where(t < partner_ref[t], t, nxt)
        following[t] = nxt
        return nxt

    lax.fori_loop(0, TILES, look_back, jnp.int32(0))

    def list_first(k, t):
        low_tile = following[t]
        first[k] = low_tile
        return low_tile + 1

    lax.fori_loop(0, PAIRS, list_first, jnp.int32(0))

    for j in range(NX):
        for l in range(SLOTS):
            for dz in range(NZ):
                pick[2 * dz * NX * SLOTS + j * SLOTS + l] = rank[ids_ref[l, vir_at(j, dz, 0)]]
        for way in range(2):
            for i in range(THIRD):
                for dz in range(NZ):
                    pick[(2 * dz + 1) * NX * SLOTS + (way * NX + j) * THIRD + i] = rank[
                        ids_ref[way * THIRD + i, vir_at(j, dz, 1 - 2 * way)]
                    ]

    def differences(q):
        kept[q].wait()
        arrived = chunks[q].at[0 : TILES - 1]
        pltpu.make_async_copy(arrived, arrived, p1_recv.at[q]).wait()

        @pl.loop(0, PAIRS)
        def _(k):
            tile = first[k]
            ring[q][k] = (
                chunks[q][tile].astype(jnp.float32) - chunks[q][partner_ref[tile]].astype(jnp.float32)
            ).astype(jnp.bfloat16)

    sent = []

    def send(src, dst, send_sem, recv_sem, to):
        copy = pltpu.make_async_remote_copy(
            src_ref=src, dst_ref=dst, send_sem=send_sem, recv_sem=recv_sem, device_id=to, device_id_type=MESH
        )
        copy.start()
        return copy

    def arrival(dst, sem):
        pltpu.make_async_copy(dst, dst, sem).wait()

    up, down = (vir_at(0, 0, 1), occ), (vir_at(0, 0, -1), occ)

    def at_place(h, way, step, q):
        return ring[(h * 7 + (0 if step == 0 else 2 * step - 1 + way)) * 2 + q]

    def pass_on(h, step, q):
        for way in range(2):
            i = ((h * 3 + step) * 2 + way) * 2 + q
            sent.append(
                send(
                    at_place(h, way, step, q), at_place(h, way, step + 1, q),
                    y_send.at[i], y_recv.at[i], (up, down)[way],
                )
            )

    def await_step(h, step, q):
        if step == 0:
            arrival(at_place(h, 0, 0, q), z_recv.at[q])
            return
        for way in range(2):
            arrival(at_place(h, way, step, q), y_recv.at[((h * 3 + step - 1) * 2 + way) * 2 + q])

    def target(h, s, q):
        rows = pl.ds(pl.multiple_of(s * PLACE + x * BLOCK, BLOCK), BLOCK)
        return sources.at[2 * h + q, rows]

    def slot(l):
        return slice(l * QUARTER, (l + 1) * QUARTER)

    def deal(h, s, q):
        i = (h * 7 + s) * 2 + q
        block, out = ring[i], picked[i]
        for j in range(1, NX):
            for l in range(SLOTS):
                out[j - 1, :, slot(l)] = block[pick[j * SLOTS + l]]
            send(
                out.at[j - 1], target(h, s, q), x_send.at[i], x_recv.at[(h * 8 + s) * 2 + q],
                (vir_at(j, 0, 0), occ),
            )
        for l in range(SLOTS):
            target(h, s, q)[:, slot(l)] = block[pick[l]]

    def deal_far(h, way, q, dz=0):
        block, out = ring[(h * 7 + 5 + way) * 2 + q], far[(h + dz) * 2 + q]
        for j in range(NX):
            for i in range(THIRD):
                out[way, j, :, slot(i)] = block[pick[(2 * dz + 1) * NX * SLOTS + (way * NX + j) * THIRD + i]]
            send(
                out.at[way, j], target(h + dz, 7, q).at[:, way * THIRD * QUARTER : (way + 1) * THIRD * QUARTER],
                far_send.at[((h + dz) * 2 + way) * 2 + q], x_recv.at[((h + dz) * 8 + 7) * 2 + q],
                (vir_at(j, dz, 1 - 2 * way), occ),
            )

    def deal_across(way):
        block, out = ring[(5 + way) * 2 + 1], across[way]
        for j in range(NX):
            for l in range(SLOTS):
                out[j, :, slot(l)] = block[pick[2 * NX * SLOTS + j * SLOTS + l]]
            send(
                out.at[j], target(1, 5 + way, 1), x_send.at[(12 + way) * 2 + 1],
                x_recv.at[(13 + way) * 2 + 1], (vir_at(j, 1, 0), occ),
            )

    def deal_step(h, step, q):
        if step == 3:
            deal_far(h, 0, q)
            deal_far(h, 1, q)
        if step == 0:
            deal(h, 0, q)
        else:
            deal(h, 2 * step - 1, q)
            deal(h, 2 * step, q)
        if (h, step, q) == (0, 3, 1):
            for way in range(2):
                deal_across(way)
                deal_far(0, way, 1, dz=1)

    def prepare_projector():
        proj_t[...] = jnp.zeros_like(proj_t)
        for o in range(NO):
            proj_t[PAD * o : PAD * o + SHARE, :] = proj_ref[SHARE * o : SHARE * (o + 1), :]
        row = lax.broadcasted_iota(jnp.int32, (ROWS, LAST), 0)
        column = lax.broadcasted_iota(jnp.int32, (ROWS, LAST), 1)
        into = jnp.zeros((ROWS, LAST), jnp.int32)
        for i in range(LAST // BLOCK):
            b = NEAR // BLOCK + i
            into = jnp.where((column >= i * BLOCK) & (column < (i + 1) * BLOCK), row_of(b) - i * BLOCK, into)
        chosen = (row == column + into).astype(jnp.bfloat16)
        proj_last[...] = jnp.dot(proj_t[...], chosen, preferred_element_type=jnp.float32).astype(jnp.bfloat16)
        for i in range(LAST // BLOCK):
            rows = pl.ds(row_of(NEAR // BLOCK + i), BLOCK)
            out_ref[0, rows, :] = jnp.zeros((BLOCK, COLS), jnp.bfloat16)
            low[rows, :] = jnp.zeros((BLOCK, COLS), jnp.bfloat16)

    def prepare_base(i):
        rows = slice(128 * i, 128 * (i + 1))
        column = jnp.broadcast_to(occ_ref[:, rows], (128, 128)).T
        wide = jnp.concatenate([column] * (COLS // 128), axis=1)
        couple = lax.dot_general(
            coup_ref[:, rows], da_ref[...], (((0,), (0,)), ((), ())), preferred_element_type=jnp.float32
        )
        base[rows, :] = couple + (ven_ref[...] - wide) * t_ref[rows, :].astype(jnp.float32)

    def prepare_ladder(l):
        tile = ids_ref[l, vir]
        sign = jnp.where(tile < partner_ref[tile], 1.0, -1.0)
        factor = jnp.where(l < len_ref[vir], sign, 0.0).astype(jnp.float32)
        for quarter in range(2 * NZ):
            plane = zh if quarter < 2 else 1 - zh
            rows = pl.ds(pl.multiple_of(plane * HALF + quarter % 2 * QUARTER, QUARTER), QUARTER)
            weights[quarter, slot(l), :] = (ladder[l, rows, :].astype(jnp.float32) * factor).astype(jnp.bfloat16)

    def row_of(b):
        s, bx = b // NX, b % NX
        offset = (s // 2) * (1 - s % 2) - ((s + 1) // 2) * (s % 2)
        return pl.multiple_of(bx * (NY * BLOCK) + lax.rem(y + offset + NY, NY) * BLOCK, BLOCK)

    def multiply(begin, end, h):
        total = jnp.zeros((end - begin, COLS), jnp.float32) if h == 0 else acc[begin:end]
        for s in range(begin // PLACE, end // PLACE):
            for q in range(2):
                i = h * 2 + q
                came = far[i] if s == 7 else across[s - 5] if i == 3 and s >= 5 else picked[(h * 7 + s) * 2 + q]
                arrival(came, x_recv.at[(h * 8 + s) * 2 + q])
        for q in range(2):
            quarter = 2 * h + q
            total += jnp.dot(sources[quarter, begin:end, :], weights[quarter], preferred_element_type=jnp.float32)
        acc[begin:end] = total

    def finish(b):
        rows = pl.ds(row_of(b), BLOCK)
        total = base[rows, :] + acc[pl.ds(pl.multiple_of(b * BLOCK, BLOCK), BLOCK), :]
        high = total.astype(jnp.bfloat16)
        out_ref[0, rows, :] = high
        return rows, high, (total - high.astype(jnp.float32)).astype(jnp.bfloat16)

    def finish_near(begin, end):
        @pl.loop(begin // BLOCK, end // BLOCK)
        def _(b):
            rows, _, rest = finish(b)
            low[rows, :] = rest

    for q in range(2):
        differences(q)
        pass_on(0, 0, q)
        sent.append(send(ring[q], ring[14 + q], z_send.at[q], z_recv.at[q], (vir_at(0, 1, 0), occ)))
    for q in range(2):
        deal_step(0, 0, q)
    for load in loads[3:]:
        load.wait()

    for h, step in ((0, 1), (0, 2), (1, 0), (0, 3), (1, 1), (1, 2), (1, 3)):
        by_ring = range(1) if (h, step) == (1, 3) else range(2)
        for q in by_ring:
            await_step(h, step, q)
            if step < 3 and not (h == 1 and step == 2 and q == 1):
                pass_on(h, step, q)
            if step == 3:
                deal_step(h, step, q)
        if step < 3:
            for q in range(2):
                deal_step(h, step, q)
        if (h, step) == (0, 1):
            prepare_projector()
        elif (h, step) == (0, 2):
            for i in range(4):
                prepare_base(i)
        elif (h, step) == (1, 0):
            for l in range(SLOTS):
                prepare_ladder(l)
        elif (h, step) == (1, 1):
            multiply(0, ROWS, 0)
        elif (h, step) == (1, 2):
            multiply(0, EARLY, 1)
            finish_near(0, EARLY)

    multiply(EARLY, NEAR, 1)
    finish_near(EARLY, NEAR)
    near[...] = jnp.dot(proj_t[...], out_ref[0], preferred_element_type=jnp.float32) + jnp.dot(
        proj_t[...], low[...], preferred_element_type=jnp.float32
    )
    multiply(NEAR, ROWS, 1)

    @pl.loop(0, LAST // BLOCK)
    def _(i):
        _, high, rest = finish(NEAR // BLOCK + i)
        rows = pl.ds(pl.multiple_of(i * BLOCK, BLOCK), BLOCK)
        last[0, rows, :] = high
        last[1, rows, :] = rest

    both = (
        near[...]
        + jnp.dot(proj_last[...], last[0], preferred_element_type=jnp.float32)
        + jnp.dot(proj_last[...], last[1], preferred_element_type=jnp.float32)
    )
    for o in range(NO):
        mine = both[PAD * o : PAD * (o + 1), :]
        rest = [mine[4 * m : 4 * (m + 1), FOLD:] for m in range(3)]
        part[o] = jnp.concatenate(
            [mine[0:SHARE, 0:FOLD], jnp.concatenate(rest, axis=1)], axis=0
        ).astype(jnp.bfloat16)

    @pl.loop(1, NO)
    def _(j):
        to = lax.rem(occ + j, NO)
        send(part.at[to], got.at[j - 1], o_send, o_recv, (vir, to))

    arrival(got, o_recv)
    total = part[occ].astype(jnp.float32)
    for j in range(NO - 1):
        total = total + got[j].astype(jnp.float32)
    out2_ref[:, 0, 0:FOLD] = total[0:SHARE, :]
    for m in range(3):
        out2_ref[4 * m : 4 * (m + 1), 0, FOLD:] = total[SHARE:, 128 * m : 128 * (m + 1)]

    for copy in sent:
        copy.wait_send()
    for q in range(2):
        arrived = chunks[q].at[0 : TILES - 1]
        pltpu.make_async_copy(arrived, arrived, p1_send.at[q]).wait()
    for i in range(28):
        dealt = across[i // 2 - 12] if i in (25, 27) else picked[i]
        pltpu.make_async_copy(dealt, dealt, x_send.at[i]).wait()
    for i in range(8):
        h, way, q = i // 4, (i // 2) % 2, i % 2
        dealt = far[h * 2 + q].at[way]
        pltpu.make_async_copy(dealt, dealt, far_send.at[i]).wait()
    pltpu.make_async_copy(got, got, o_send).wait()


def on_device(
    triple_amps, double_amps, ladder_block_table, source_ids, list_length, partner, virtual_energy,
    triple_occupied_energy, coupling, projector,
):
    vmem, hbm = pl.BlockSpec(memory_space=pltpu.VMEM), pl.BlockSpec(memory_space=pltpu.HBM)
    bf16, f32, i32 = jnp.bfloat16, jnp.float32, jnp.int32
    dma = pltpu.SemaphoreType.DMA
    arrays = (
        triple_amps, double_amps, ladder_block_table, source_ids.T, list_length, partner, virtual_energy,
        triple_occupied_energy.reshape(1, ROWS), coupling.T, projector.T,
    )
    sigma_triples, sigma_doubles = pl.pallas_call(
        kernel,
        out_shape=(
            jax.ShapeDtypeStruct((1, ROWS, COLS), bf16),
            jax.ShapeDtypeStruct((SHARE, 1, COLS), f32),
        ),
        in_specs=[hbm] * len(arrays),
        out_specs=(vmem, vmem),
        scratch_shapes=[
            pltpu.VMEM((ROWS, COLS), bf16),
            pltpu.VMEM((OCCJ, COLS), bf16),
            pltpu.SMEM((SLOTS, TILES), i32),
            pltpu.SMEM((TILES,), i32),
            pltpu.SMEM((TILES,), i32),
            pltpu.VMEM((1, COLS), f32),
            pltpu.VMEM((1, ROWS), f32),
            pltpu.VMEM((OCCJ, ROWS), bf16),
            pltpu.VMEM((OCCJ, ROWS), bf16),
            pltpu.VMEM((SLOTS, COLS, COLS), bf16),
            [pltpu.VMEM((TILES, BLOCK, QUARTER), bf16)] * 2,
            [pltpu.VMEM((PAIRS, BLOCK, QUARTER), bf16)] * 28,
            [pltpu.VMEM((NX - 1, BLOCK, SLOTS * QUARTER), bf16)] * 28,
            [pltpu.VMEM((NX, BLOCK, SLOTS * QUARTER), bf16)] * 2,
            [pltpu.VMEM((2, NX, BLOCK, THIRD * QUARTER), bf16)] * 4,
            pltpu.VMEM((2 * NZ, ROWS, SLOTS * QUARTER), bf16),
            pltpu.VMEM((2 * NZ, SLOTS * QUARTER, COLS), bf16),
            pltpu.VMEM((ROWS, COLS), f32),
            pltpu.VMEM((ROWS, COLS), f32),
            pltpu.VMEM((ROWS, COLS), bf16),
            pltpu.VMEM((2, LAST, COLS), bf16),
            pltpu.VMEM((NO * PAD, COLS), f32),
            pltpu.VMEM((NO * PAD, ROWS), bf16),
            pltpu.VMEM((NO * PAD, LAST), bf16),
            pltpu.VMEM((NO, PAD, FOLD), bf16),
            pltpu.VMEM((NO - 1, PAD, FOLD), bf16),
            pltpu.SMEM((TILES,), jnp.int32),
            pltpu.SMEM((TILES + 1,), jnp.int32),
            pltpu.SMEM((PAIRS,), jnp.int32),
            pltpu.SMEM((4 * NX * SLOTS,), jnp.int32),
            dma((10,)), dma((2,)), dma((2,)), dma((2,)), dma((2,)), dma((2,)),
            dma((24,)), dma((24,)), dma((28,)), dma((32,)), dma((8,)),
            dma, dma,
        ],
        compiler_params=pltpu.CompilerParams(
            collective_id=0, has_side_effects=True, vmem_limit_bytes=48 * 1024 * 1024
        ),
        name="sigma",
    )(*(pltpu.with_memory_space_constraint(a, pltpu.HBM) for a in arrays))
    return sigma_triples, jnp.swapaxes(sigma_doubles, 0, 1)


def solution(mesh):
    return jax.shard_map(
        on_device,
        mesh=mesh,
        in_specs=(
            P("vir", "occ", None),
            P("vir", None, None),
            P("vir", None, None, None),
            P(),
            P(),
            P(),
            P("vir", None),
            P("occ"),
            P("occ", None),
            P("occ", None),
        ),
        out_specs=(P("vir", "occ", None), P("vir", "occ", None)),
        check_vma=False,
    )
```

```python
import jax
import jax.numpy as jnp
from jax import lax
from jax.experimental import pallas as pl
from jax.experimental.pallas import tpu as pltpu
from jax.sharding import PartitionSpec as P

MESH = pl.DeviceIdType.MESH

NX, NZ, NY, NO = 4, 2, 8, 8
TILES = NX * NZ * NY
PAIRS = TILES // 2
SLOTS = 6
ROWS = 512
COLS = 512
BLOCK = ROWS // (NX * NY)
HALF = COLS // NZ
OCCJ = 96
SHARE = OCCJ // NO
PAD = 16
QUARTER = HALF // 2
OFFSETS = (0, -1, 1, -2, 2, -3, 3, 4)
PLACE = NX * BLOCK
EARLY = 3 * PLACE
NEAR = 5 * PLACE
LAST = 3 * PLACE
THIRD = SLOTS // 2
FOLD = 384


def kernel(
    t_hbm, da_hbm, ladder_hbm, ids_hbm, len_hbm, partner_hbm, ven_hbm, occ_hbm, coup_hbm, proj_hbm,
    out_ref, out2_ref,
    t_ref, da_ref, ids_ref, len_ref, partner_ref, ven_ref, occ_ref, coup_ref, proj_ref,
    ladder, chunks, ring, picked, across, far, sources, weights, acc, base, low, last, near, proj_t, proj_last, part, got,
    rank, following, first, pick,
    load_sem, p1_send, p1_recv, own_sem, z_send, z_recv, y_send, y_recv, x_send, x_recv, far_send, o_send, o_recv,
):
    vir, occ = lax.axis_index("vir"), lax.axis_index("occ")
    x, zh, y = vir // (NZ * NY), (vir // NY) % NZ, vir % NY

    def vir_at(dx, dz, dy):
        return ((x + dx) % NX) * (NZ * NY) + ((zh + dz) % NZ) * NY + (y + dy) % NY

    barrier = pltpu.get_barrier_semaphore()

    def in_vir(vx, vz, vy):
        return (vx * (NZ * NY) + vz * NY + vy, occ)

    def for_others(act):
        act(x, 1 - zh, y)
        for dx in range(NX):
            vx = lax.rem(x + dx, NX)

            @pl.loop(0 if dx else 1, NY)
            def _(dy, vx=vx):
                vy = lax.rem(y + dy, NY)
                act(vx, 1 - zh, vy)
                act(vx, zh, vy)

    def greet(*at):
        pl.semaphore_signal(barrier, inc=1, device_id=in_vir(*at), device_id_type=MESH)

    for_others(greet)

    @pl.loop(1, NO)
    def _(j):
        pl.semaphore_signal(barrier, inc=1, device_id=(vir, lax.rem(occ + j, NO)), device_id_type=MESH)

    loads = [
        pltpu.make_async_copy(src, dst, load_sem.at[i])
        for i, (src, dst) in enumerate((
            (partner_hbm, partner_ref), (ids_hbm, ids_ref), (len_hbm, len_ref), (occ_hbm, occ_ref),
            (proj_hbm, proj_ref), (coup_hbm, coup_ref), (da_hbm.at[0], da_ref), (ven_hbm, ven_ref),
            (t_hbm.at[0], t_ref), (ladder_hbm.at[0], ladder),
        ))
    ]
    for load in loads:
        load.start()

    pl.semaphore_wait(barrier, TILES + NO - 2)

    def chunk_of(vx, vz, vy, q):
        return t_hbm.at[
            0,
            pl.ds(pl.multiple_of(vx * (NY * BLOCK) + vy * BLOCK, BLOCK), BLOCK),
            pl.ds(pl.multiple_of(vz * HALF + q * QUARTER, QUARTER), QUARTER),
        ]

    def spread(q):
        def to(*at):
            pltpu.make_async_remote_copy(
                src_ref=chunk_of(*at, q), dst_ref=chunks[q].at[vir], send_sem=p1_send.at[q], recv_sem=p1_recv.at[q],
                device_id=in_vir(*at), device_id_type=MESH,
            ).start()

        for_others(to)
        keep = pltpu.make_async_copy(chunk_of(x, zh, y, q), chunks[q].at[vir], own_sem.at[q])
        keep.start()
        return keep

    kept = [spread(q) for q in range(2)]

    for load in loads[:3]:
        load.wait()

    @pl.loop(0, TILES)
    def _(t):
        rank[t] = 0

    def number(t, count):
        other = partner_ref[t]
        lower = t < other
        rank[t] = jnp.where(lower, count, rank[other])
        return count + lower.astype(jnp.int32)

    lax.fori_loop(0, TILES, number, jnp.int32(0))
    following[TILES] = 0

    def look_back(i, nxt):
        t = TILES - 1 - i
        nxt = jnp.where(t < partner_ref[t], t, nxt)
        following[t] = nxt
        return nxt

    lax.fori_loop(0, TILES, look_back, jnp.int32(0))

    def list_first(k, t):
        low_tile = following[t]
        first[k] = low_tile
        return low_tile + 1

    lax.fori_loop(0, PAIRS, list_first, jnp.int32(0))

    for j in range(NX):
        for l in range(SLOTS):
            for dz in range(NZ):
                pick[2 * dz * NX * SLOTS + j * SLOTS + l] = rank[ids_ref[l, vir_at(j, dz, 0)]]
        for way in range(2):
            for i in range(THIRD):
                for dz in range(NZ):
                    pick[(2 * dz + 1) * NX * SLOTS + (way * NX + j) * THIRD + i] = rank[
                        ids_ref[way * THIRD + i, vir_at(j, dz, 1 - 2 * way)]
                    ]

    def differences(q):
        kept[q].wait()
        arrived = chunks[q].at[0 : TILES - 1]
        pltpu.make_async_copy(arrived, arrived, p1_recv.at[q]).wait()

        @pl.loop(0, PAIRS)
        def _(k):
            tile = first[k]
            ring[q][k] = (
                chunks[q][tile].astype(jnp.float32) - chunks[q][partner_ref[tile]].astype(jnp.float32)
            ).astype(jnp.bfloat16)

    sent = []

    def send(src, dst, send_sem, recv_sem, to):
        copy = pltpu.make_async_remote_copy(
            src_ref=src, dst_ref=dst, send_sem=send_sem, recv_sem=recv_sem, device_id=to, device_id_type=MESH
        )
        copy.start()
        return copy

    def arrival(dst, sem):
        pltpu.make_async_copy(dst, dst, sem).wait()

    up, down = (vir_at(0, 0, 1), occ), (vir_at(0, 0, -1), occ)

    def at_place(h, way, step, q):
        return ring[(h * 7 + (0 if step == 0 else 2 * step - 1 + way)) * 2 + q]

    def pass_on(h, step, q):
        for way in range(2):
            i = ((h * 3 + step) * 2 + way) * 2 + q
            sent.append(
                send(
                    at_place(h, way, step, q), at_place(h, way, step + 1, q),
                    y_send.at[i], y_recv.at[i], (up, down)[way],
                )
            )

    def await_step(h, step, q):
        if step == 0:
            arrival(at_place(h, 0, 0, q), z_recv.at[q])
            return
        for way in range(2):
            arrival(at_place(h, way, step, q), y_recv.at[((h * 3 + step - 1) * 2 + way) * 2 + q])

    def target(h, s, q):
        rows = pl.ds(pl.multiple_of(s * PLACE + x * BLOCK, BLOCK), BLOCK)
        return sources.at[2 * h + q, rows]

    def slot(l):
        return slice(l * QUARTER, (l + 1) * QUARTER)

    def deal(h, s, q):
        i = (h * 7 + s) * 2 + q
        block, out = ring[i], picked[i]
        for j in range(1, NX):
            for l in range(SLOTS):
                out[j - 1, :, slot(l)] = block[pick[j * SLOTS + l]]
            send(
                out.at[j - 1], target(h, s, q), x_send.at[i], x_recv.at[(h * 8 + s) * 2 + q],
                (vir_at(j, 0, 0), occ),
            )
        for l in range(SLOTS):
            target(h, s, q)[:, slot(l)] = block[pick[l]]

    def deal_far(h, way, q, dz=0):
        block, out = ring[(h * 7 + 5 + way) * 2 + q], far[(h + dz) * 2 + q]
        for j in range(NX):
            for i in range(THIRD):
                out[way, j, :, slot(i)] = block[pick[(2 * dz + 1) * NX * SLOTS + (way * NX + j) * THIRD + i]]
            send(
                out.at[way, j], target(h + dz, 7, q).at[:, way * THIRD * QUARTER : (way + 1) * THIRD * QUARTER],
                far_send.at[((h + dz) * 2 + way) * 2 + q], x_recv.at[((h + dz) * 8 + 7) * 2 + q],
                (vir_at(j, dz, 1 - 2 * way), occ),
            )

    def deal_across(way):
        block, out = ring[(5 + way) * 2 + 1], across[way]
        for j in range(NX):
            for l in range(SLOTS):
                out[j, :, slot(l)] = block[pick[2 * NX * SLOTS + j * SLOTS + l]]
            send(
                out.at[j], target(1, 5 + way, 1), x_send.at[(12 + way) * 2 + 1],
                x_recv.at[(13 + way) * 2 + 1], (vir_at(j, 1, 0), occ),
            )

    def deal_step(h, step, q):
        if step == 3:
            deal_far(h, 0, q)
            deal_far(h, 1, q)
        if step == 0:
            deal(h, 0, q)
        else:
            deal(h, 2 * step - 1, q)
            deal(h, 2 * step, q)
        if (h, step, q) == (0, 3, 1):
            for way in range(2):
                deal_across(way)
                deal_far(0, way, 1, dz=1)

    def prepare_projector():
        proj_t[...] = jnp.zeros_like(proj_t)
        for o in range(NO):
            proj_t[PAD * o : PAD * o + SHARE, :] = proj_ref[SHARE * o : SHARE * (o + 1), :]
        row = lax.broadcasted_iota(jnp.int32, (ROWS, LAST), 0)
        column = lax.broadcasted_iota(jnp.int32, (ROWS, LAST), 1)
        into = jnp.zeros((ROWS, LAST), jnp.int32)
        for i in range(LAST // BLOCK):
            b = NEAR // BLOCK + i
            into = jnp.where((column >= i * BLOCK) & (column < (i + 1) * BLOCK), row_of(b) - i * BLOCK, into)
        chosen = (row == column + into).astype(jnp.bfloat16)
        proj_last[...] = jnp.dot(proj_t[...], chosen, preferred_element_type=jnp.float32).astype(jnp.bfloat16)
        for i in range(LAST // BLOCK):
            rows = pl.ds(row_of(NEAR // BLOCK + i), BLOCK)
            out_ref[0, rows, :] = jnp.zeros((BLOCK, COLS), jnp.bfloat16)
            low[rows, :] = jnp.zeros((BLOCK, COLS), jnp.bfloat16)

    def prepare_base(i):
        rows = slice(128 * i, 128 * (i + 1))
        column = jnp.broadcast_to(occ_ref[:, rows], (128, 128)).T
        wide = jnp.concatenate([column] * (COLS // 128), axis=1)
        couple = lax.dot_general(
            coup_ref[:, rows], da_ref[...], (((0,), (0,)), ((), ())), preferred_element_type=jnp.float32
        )
        base[rows, :] = couple + (ven_ref[...] - wide) * t_ref[rows, :].astype(jnp.float32)

    def prepare_ladder(l):
        tile = ids_ref[l, vir]
        sign = jnp.where(tile < partner_ref[tile], 1.0, -1.0)
        factor = jnp.where(l < len_ref[vir], sign, 0.0).astype(jnp.float32)
        for quarter in range(2 * NZ):
            plane = zh if quarter < 2 else 1 - zh
            rows = pl.ds(pl.multiple_of(plane * HALF + quarter % 2 * QUARTER, QUARTER), QUARTER)
            weights[quarter, slot(l), :] = (ladder[l, rows, :].astype(jnp.float32) * factor).astype(jnp.bfloat16)

    def row_of(b):
        s, bx = b // NX, b % NX
        offset = (s // 2) * (1 - s % 2) - ((s + 1) // 2) * (s % 2)
        return pl.multiple_of(bx * (NY * BLOCK) + lax.rem(y + offset + NY, NY) * BLOCK, BLOCK)

    def multiply(begin, end, h):
        total = jnp.zeros((end - begin, COLS), jnp.float32) if h == 0 else acc[begin:end]
        for q in (1, 0):
            quarter = 2 * h + q
            for s in range(begin // PLACE, end // PLACE):
                came = far[quarter] if s == 7 else across[s - 5] if quarter == 3 and s >= 5 else picked[(h * 7 + s) * 2 + q]
                arrival(came, x_recv.at[(h * 8 + s) * 2 + q])
            total += jnp.dot(sources[quarter, begin:end, :], weights[quarter], preferred_element_type=jnp.float32)
        acc[begin:end] = total

    def finish(b):
        rows = pl.ds(row_of(b), BLOCK)
        total = base[rows, :] + acc[pl.ds(pl.multiple_of(b * BLOCK, BLOCK), BLOCK), :]
        high = total.astype(jnp.bfloat16)
        out_ref[0, rows, :] = high
        return rows, high, (total - high.astype(jnp.float32)).astype(jnp.bfloat16)

    def finish_near(begin, end):
        @pl.loop(begin // BLOCK, end // BLOCK)
        def _(b):
            rows, _, rest = finish(b)
            low[rows, :] = rest

    for q in range(2):
        differences(q)
        sent.append(send(ring[q], ring[14 + q], z_send.at[q], z_recv.at[q], (vir_at(0, 1, 0), occ)))
        pass_on(0, 0, q)
    for q in range(2):
        deal_step(0, 0, q)
    for load in loads[3:]:
        load.wait()

    for h, step in ((0, 1), (0, 2), (1, 0), (0, 3), (1, 1), (1, 2), (1, 3)):
        by_ring = range(1) if (h, step) == (1, 3) else range(2)
        for q in by_ring:
            await_step(h, step, q)
            if step < 3 and not (h == 1 and step == 2 and q == 1):
                pass_on(h, step, q)
            if step == 3:
                deal_step(h, step, q)
        if step < 3:
            for q in range(2):
                deal_step(h, step, q)
        if (h, step) == (0, 1):
            prepare_projector()
        elif (h, step) == (0, 2):
            for i in range(4):
                prepare_base(i)
        elif (h, step) == (1, 0):
            for l in range(SLOTS):
                prepare_ladder(l)
        elif (h, step) == (0, 3):
            multiply(0, NEAR, 0)
        elif (h, step) == (1, 1):
            multiply(NEAR, ROWS, 0)
        elif (h, step) == (1, 2):
            multiply(0, EARLY, 1)
            finish_near(0, EARLY)

    multiply(EARLY, NEAR, 1)
    finish_near(EARLY, NEAR)
    near[...] = jnp.dot(proj_t[...], out_ref[0], preferred_element_type=jnp.float32) + jnp.dot(
        proj_t[...], low[...], preferred_element_type=jnp.float32
    )
    multiply(NEAR, ROWS, 1)

    @pl.loop(0, LAST // BLOCK)
    def _(i):
        _, high, rest = finish(NEAR // BLOCK + i)
        rows = pl.ds(pl.multiple_of(i * BLOCK, BLOCK), BLOCK)
        last[0, rows, :] = high
        last[1, rows, :] = rest

    both = (
        near[...]
        + jnp.dot(proj_last[...], last[0], preferred_element_type=jnp.float32)
        + jnp.dot(proj_last[...], last[1], preferred_element_type=jnp.float32)
    )
    for o in range(NO):
        mine = both[PAD * o : PAD * (o + 1), :]
        rest = [mine[4 * m : 4 * (m + 1), FOLD:] for m in range(3)]
        part[o] = jnp.concatenate(
            [mine[0:SHARE, 0:FOLD], jnp.concatenate(rest, axis=1)], axis=0
        ).astype(jnp.bfloat16)

    @pl.loop(1, NO)
    def _(j):
        to = lax.rem(occ + j, NO)
        send(part.at[to], got.at[j - 1], o_send, o_recv, (vir, to))

    for copy in sent:
        copy.wait_send()
    for q in range(2):
        arrived = chunks[q].at[0 : TILES - 1]
        pltpu.make_async_copy(arrived, arrived, p1_send.at[q]).wait()
    for i in range(28):
        dealt = across[i // 2 - 12] if i in (25, 27) else picked[i]
        pltpu.make_async_copy(dealt, dealt, x_send.at[i]).wait()
    for i in range(8):
        h, way, q = i // 4, (i // 2) % 2, i % 2
        dealt = far[h * 2 + q].at[way]
        pltpu.make_async_copy(dealt, dealt, far_send.at[i]).wait()
    arrival(got, o_recv)
    total = part[occ].astype(jnp.float32)
    for j in range(NO - 1):
        total = total + got[j].astype(jnp.float32)
    out2_ref[:, 0, 0:FOLD] = total[0:SHARE, :]
    for m in range(3):
        out2_ref[4 * m : 4 * (m + 1), 0, FOLD:] = total[SHARE:, 128 * m : 128 * (m + 1)]

    pltpu.make_async_copy(got, got, o_send).wait()


def on_device(
    triple_amps, double_amps, ladder_block_table, source_ids, list_length, partner, virtual_energy,
    triple_occupied_energy, coupling, projector,
):
    vmem, hbm = pl.BlockSpec(memory_space=pltpu.VMEM), pl.BlockSpec(memory_space=pltpu.HBM)
    bf16, f32, i32 = jnp.bfloat16, jnp.float32, jnp.int32
    dma = pltpu.SemaphoreType.DMA
    arrays = (
        triple_amps, double_amps, ladder_block_table, source_ids.T, list_length, partner, virtual_energy,
        triple_occupied_energy.reshape(1, ROWS), coupling.T, projector.T,
    )
    sigma_triples, sigma_doubles = pl.pallas_call(
        kernel,
        out_shape=(
            jax.ShapeDtypeStruct((1, ROWS, COLS), bf16),
            jax.ShapeDtypeStruct((SHARE, 1, COLS), f32),
        ),
        in_specs=[hbm] * len(arrays),
        out_specs=(vmem, vmem),
        scratch_shapes=[
            pltpu.VMEM((ROWS, COLS), bf16),
            pltpu.VMEM((OCCJ, COLS), bf16),
            pltpu.SMEM((SLOTS, TILES), i32),
            pltpu.SMEM((TILES,), i32),
            pltpu.SMEM((TILES,), i32),
            pltpu.VMEM((1, COLS), f32),
            pltpu.VMEM((1, ROWS), f32),
            pltpu.VMEM((OCCJ, ROWS), bf16),
            pltpu.VMEM((OCCJ, ROWS), bf16),
            pltpu.VMEM((SLOTS, COLS, COLS), bf16),
            [pltpu.VMEM((TILES, BLOCK, QUARTER), bf16)] * 2,
            [pltpu.VMEM((PAIRS, BLOCK, QUARTER), bf16)] * 28,
            [pltpu.VMEM((NX - 1, BLOCK, SLOTS * QUARTER), bf16)] * 28,
            [pltpu.VMEM((NX, BLOCK, SLOTS * QUARTER), bf16)] * 2,
            [pltpu.VMEM((2, NX, BLOCK, THIRD * QUARTER), bf16)] * 4,
            pltpu.VMEM((2 * NZ, ROWS, SLOTS * QUARTER), bf16),
            pltpu.VMEM((2 * NZ, SLOTS * QUARTER, COLS), bf16),
            pltpu.VMEM((ROWS, COLS), f32),
            pltpu.VMEM((ROWS, COLS), f32),
            pltpu.VMEM((ROWS, COLS), bf16),
            pltpu.VMEM((2, LAST, COLS), bf16),
            pltpu.VMEM((NO * PAD, COLS), f32),
            pltpu.VMEM((NO * PAD, ROWS), bf16),
            pltpu.VMEM((NO * PAD, LAST), bf16),
            pltpu.VMEM((NO, PAD, FOLD), bf16),
            pltpu.VMEM((NO - 1, PAD, FOLD), bf16),
            pltpu.SMEM((TILES,), jnp.int32),
            pltpu.SMEM((TILES + 1,), jnp.int32),
            pltpu.SMEM((PAIRS,), jnp.int32),
            pltpu.SMEM((4 * NX * SLOTS,), jnp.int32),
            dma((10,)), dma((2,)), dma((2,)), dma((2,)), dma((2,)), dma((2,)),
            dma((24,)), dma((24,)), dma((28,)), dma((32,)), dma((8,)),
            dma, dma,
        ],
        compiler_params=pltpu.CompilerParams(
            collective_id=0, has_side_effects=True, vmem_limit_bytes=48 * 1024 * 1024
        ),
        name="sigma",
    )(*(pltpu.with_memory_space_constraint(a, pltpu.HBM) for a in arrays))
    return sigma_triples, jnp.swapaxes(sigma_doubles, 0, 1)


def solution(mesh):
    return jax.shard_map(
        on_device,
        mesh=mesh,
        in_specs=(
            P("vir", "occ", None),
            P("vir", None, None),
            P("vir", None, None, None),
            P(),
            P(),
            P(),
            P("vir", None),
            P("occ"),
            P("occ", None),
            P("occ", None),
        ),
        out_specs=(P("vir", "occ", None), P("vir", "occ", None)),
        check_vma=False,
    )
```

```python
import jax
import jax.numpy as jnp
from jax import lax
from jax.experimental import pallas as pl
from jax.experimental.pallas import tpu as pltpu
from jax.sharding import PartitionSpec as P

MESH = pl.DeviceIdType.MESH

NX, NZ, NY, NO = 4, 2, 8, 8
TILES = NX * NZ * NY
PAIRS = TILES // 2
SLOTS = 6
ROWS = 512
COLS = 512
BLOCK = ROWS // (NX * NY)
HALF = COLS // NZ
OCCJ = 96
SHARE = OCCJ // NO
PAD = 16
QUARTER = HALF // 2
OFFSETS = (0, -1, 1, -2, 2, -3, 3, 4)
PLACE = NX * BLOCK
EARLY = 3 * PLACE
NEAR = 5 * PLACE
LAST = 3 * PLACE
THIRD = SLOTS // 2
FOLD = 384


def kernel(
    t_hbm, da_hbm, ladder_hbm, ids_hbm, len_hbm, partner_hbm, ven_hbm, occ_hbm, coup_hbm, proj_hbm,
    out_ref, out2_ref,
    t_ref, da_ref, ids_ref, len_ref, partner_ref, ven_ref, occ_ref, coup_ref, proj_ref,
    ladder, chunks, ring, picked, across, far, sources, weights, acc, base, low, last, near, proj_t, proj_last, part, got,
    rank, following, first, pick,
    load_sem, p1_send, p1_recv, own_sem, z_send, z_recv, y_send, y_recv, x_send, x_recv, far_send, o_send, o_recv,
):
    vir, occ = lax.axis_index("vir"), lax.axis_index("occ")
    x, zh, y = vir // (NZ * NY), (vir // NY) % NZ, vir % NY

    def vir_at(dx, dz, dy):
        return ((x + dx) % NX) * (NZ * NY) + ((zh + dz) % NZ) * NY + (y + dy) % NY

    barrier = pltpu.get_barrier_semaphore()

    def in_vir(vx, vz, vy):
        return (vx * (NZ * NY) + vz * NY + vy, occ)

    def for_others(act):
        act(x, 1 - zh, y)
        for dx in range(NX):
            vx = lax.rem(x + dx, NX)

            @pl.loop(0 if dx else 1, NY)
            def _(dy, vx=vx):
                vy = lax.rem(y + dy, NY)
                act(vx, 1 - zh, vy)
                act(vx, zh, vy)

    def greet(*at):
        pl.semaphore_signal(barrier, inc=1, device_id=in_vir(*at), device_id_type=MESH)

    for_others(greet)

    @pl.loop(1, NO)
    def _(j):
        pl.semaphore_signal(barrier, inc=1, device_id=(vir, lax.rem(occ + j, NO)), device_id_type=MESH)

    loads = [
        pltpu.make_async_copy(src, dst, load_sem.at[i])
        for i, (src, dst) in enumerate((
            (partner_hbm, partner_ref), (ids_hbm, ids_ref), (len_hbm, len_ref), (occ_hbm, occ_ref),
            (proj_hbm, proj_ref), (coup_hbm, coup_ref), (da_hbm.at[0], da_ref), (ven_hbm, ven_ref),
            (t_hbm.at[0], t_ref), (ladder_hbm.at[0], ladder),
        ))
    ]
    for load in loads:
        load.start()

    pl.semaphore_wait(barrier, TILES + NO - 2)

    def chunk_of(vx, vz, vy, q):
        return t_hbm.at[
            0,
            pl.ds(pl.multiple_of(vx * (NY * BLOCK) + vy * BLOCK, BLOCK), BLOCK),
            pl.ds(pl.multiple_of(vz * HALF + q * QUARTER, QUARTER), QUARTER),
        ]

    def spread(q):
        def to(*at):
            pltpu.make_async_remote_copy(
                src_ref=chunk_of(*at, q), dst_ref=chunks[q].at[vir], send_sem=p1_send.at[q], recv_sem=p1_recv.at[q],
                device_id=in_vir(*at), device_id_type=MESH,
            ).start()

        for_others(to)
        keep = pltpu.make_async_copy(chunk_of(x, zh, y, q), chunks[q].at[vir], own_sem.at[q])
        keep.start()
        return keep

    kept = [spread(q) for q in range(2)]

    for load in loads[:3]:
        load.wait()

    @pl.loop(0, TILES)
    def _(t):
        rank[t] = 0

    def number(t, count):
        other = partner_ref[t]
        lower = t < other
        rank[t] = jnp.where(lower, count, rank[other])
        return count + lower.astype(jnp.int32)

    lax.fori_loop(0, TILES, number, jnp.int32(0))
    following[TILES] = 0

    def look_back(i, nxt):
        t = TILES - 1 - i
        nxt = jnp.where(t < partner_ref[t], t, nxt)
        following[t] = nxt
        return nxt

    lax.fori_loop(0, TILES, look_back, jnp.int32(0))

    def list_first(k, t):
        low_tile = following[t]
        first[k] = low_tile
        return low_tile + 1

    lax.fori_loop(0, PAIRS, list_first, jnp.int32(0))

    for j in range(NX):
        for l in range(SLOTS):
            for dz in range(NZ):
                pick[2 * dz * NX * SLOTS + j * SLOTS + l] = rank[ids_ref[l, vir_at(j, dz, 0)]]
        for way in range(2):
            for i in range(THIRD):
                for dz in range(NZ):
                    pick[(2 * dz + 1) * NX * SLOTS + (way * NX + j) * THIRD + i] = rank[
                        ids_ref[way * THIRD + i, vir_at(j, dz, 1 - 2 * way)]
                    ]

    def differences(q):
        kept[q].wait()
        arrived = chunks[q].at[0 : TILES - 1]
        pltpu.make_async_copy(arrived, arrived, p1_recv.at[q]).wait()

        @pl.loop(0, PAIRS)
        def _(k):
            tile = first[k]
            ring[q][k] = (
                chunks[q][tile].astype(jnp.float32) - chunks[q][partner_ref[tile]].astype(jnp.float32)
            ).astype(jnp.bfloat16)

    sent = []

    def send(src, dst, send_sem, recv_sem, to):
        copy = pltpu.make_async_remote_copy(
            src_ref=src, dst_ref=dst, send_sem=send_sem, recv_sem=recv_sem, device_id=to, device_id_type=MESH
        )
        copy.start()
        return copy

    def arrival(dst, sem):
        pltpu.make_async_copy(dst, dst, sem).wait()

    up, down = (vir_at(0, 0, 1), occ), (vir_at(0, 0, -1), occ)

    def at_place(h, way, step, q):
        return ring[(h * 7 + (0 if step == 0 else 2 * step - 1 + way)) * 2 + q]

    def pass_on(h, step, q):
        for way in range(2):
            i = ((h * 3 + step) * 2 + way) * 2 + q
            sent.append(
                send(
                    at_place(h, way, step, q), at_place(h, way, step + 1, q),
                    y_send.at[i], y_recv.at[i], (up, down)[way],
                )
            )

    def await_step(h, step, q):
        if step == 0:
            arrival(at_place(h, 0, 0, q), z_recv.at[q])
            return
        for way in range(2):
            arrival(at_place(h, way, step, q), y_recv.at[((h * 3 + step - 1) * 2 + way) * 2 + q])

    def target(h, s, q):
        rows = pl.ds(pl.multiple_of(s * PLACE + x * BLOCK, BLOCK), BLOCK)
        return sources.at[2 * h + q, rows]

    def slot(l):
        return slice(l * QUARTER, (l + 1) * QUARTER)

    def deal(h, s, q):
        i = (h * 7 + s) * 2 + q
        block, out = ring[i], picked[i]
        for j in range(1, NX):
            for l in range(SLOTS):
                out[j - 1, :, slot(l)] = block[pick[j * SLOTS + l]]
            send(
                out.at[j - 1], target(h, s, q), x_send.at[i], x_recv.at[(h * 8 + s) * 2 + q],
                (vir_at(j, 0, 0), occ),
            )
        for l in range(SLOTS):
            target(h, s, q)[:, slot(l)] = block[pick[l]]

    def deal_far(h, way, q, dz=0):
        block, out = ring[(h * 7 + 5 + way) * 2 + q], far[(h + dz) * 2 + q]
        for j in range(NX):
            for i in range(THIRD):
                out[way, j, :, slot(i)] = block[pick[(2 * dz + 1) * NX * SLOTS + (way * NX + j) * THIRD + i]]
            send(
                out.at[way, j], target(h + dz, 7, q).at[:, way * THIRD * QUARTER : (way + 1) * THIRD * QUARTER],
                far_send.at[((h + dz) * 2 + way) * 2 + q], x_recv.at[((h + dz) * 8 + 7) * 2 + q],
                (vir_at(j, dz, 1 - 2 * way), occ),
            )

    def deal_across(way):
        block, out = ring[(5 + way) * 2 + 1], across[way]
        for j in range(NX):
            for l in range(SLOTS):
                out[j, :, slot(l)] = block[pick[2 * NX * SLOTS + j * SLOTS + l]]
            send(
                out.at[j], target(1, 5 + way, 1), x_send.at[(12 + way) * 2 + 1],
                x_recv.at[(13 + way) * 2 + 1], (vir_at(j, 1, 0), occ),
            )

    def deal_step(h, step, q):
        if step == 3:
            deal_far(h, 0, q)
            deal_far(h, 1, q)
        if step == 0:
            deal(h, 0, q)
        else:
            deal(h, 2 * step - 1, q)
            deal(h, 2 * step, q)
        if (h, step, q) == (0, 3, 1):
            for way in range(2):
                deal_across(way)
                deal_far(0, way, 1, dz=1)

    def prepare_projector():
        proj_t[...] = jnp.zeros_like(proj_t)
        for o in range(NO):
            proj_t[PAD * o : PAD * o + SHARE, :] = proj_ref[SHARE * o : SHARE * (o + 1), :]
        row = lax.broadcasted_iota(jnp.int32, (ROWS, LAST), 0)
        column = lax.broadcasted_iota(jnp.int32, (ROWS, LAST), 1)
        into = jnp.zeros((ROWS, LAST), jnp.int32)
        for i in range(LAST // BLOCK):
            b = NEAR // BLOCK + i
            into = jnp.where((column >= i * BLOCK) & (column < (i + 1) * BLOCK), row_of(b) - i * BLOCK, into)
        chosen = (row == column + into).astype(jnp.bfloat16)
        proj_last[...] = jnp.dot(proj_t[...], chosen, preferred_element_type=jnp.float32).astype(jnp.bfloat16)
        for i in range(LAST // BLOCK):
            rows = pl.ds(row_of(NEAR // BLOCK + i), BLOCK)
            out_ref[0, rows, :] = jnp.zeros((BLOCK, COLS), jnp.bfloat16)
            low[rows, :] = jnp.zeros((BLOCK, COLS), jnp.bfloat16)

    def prepare_base(i):
        rows = slice(128 * i, 128 * (i + 1))
        column = jnp.broadcast_to(occ_ref[:, rows], (128, 128)).T
        wide = jnp.concatenate([column] * (COLS // 128), axis=1)
        couple = lax.dot_general(
            coup_ref[:, rows], da_ref[...], (((0,), (0,)), ((), ())), preferred_element_type=jnp.float32
        )
        base[rows, :] = couple + (ven_ref[...] - wide) * t_ref[rows, :].astype(jnp.float32)

    def prepare_ladder(l):
        tile = ids_ref[l, vir]
        sign = jnp.where(tile < partner_ref[tile], 1.0, -1.0)
        factor = jnp.where(l < len_ref[vir], sign, 0.0).astype(jnp.float32)
        for quarter in range(2 * NZ):
            plane = zh if quarter < 2 else 1 - zh
            rows = pl.ds(pl.multiple_of(plane * HALF + quarter % 2 * QUARTER, QUARTER), QUARTER)
            weights[quarter, slot(l), :] = (ladder[l, rows, :].astype(jnp.float32) * factor).astype(jnp.bfloat16)

    def row_of(b):
        s, bx = b // NX, b % NX
        offset = (s // 2) * (1 - s % 2) - ((s + 1) // 2) * (s % 2)
        return pl.multiple_of(bx * (NY * BLOCK) + lax.rem(y + offset + NY, NY) * BLOCK, BLOCK)

    def multiply(begin, end, h):
        total = jnp.zeros((end - begin, COLS), jnp.float32) if h == 0 else acc[begin:end]
        for q in (1, 0):
            quarter = 2 * h + q
            for s in range(begin // PLACE, end // PLACE):
                came = far[quarter] if s == 7 else across[s - 5] if quarter == 3 and s >= 5 else picked[(h * 7 + s) * 2 + q]
                arrival(came, x_recv.at[(h * 8 + s) * 2 + q])
            total += jnp.dot(sources[quarter, begin:end, :], weights[quarter], preferred_element_type=jnp.float32)
        acc[begin:end] = total

    def finish(b):
        rows = pl.ds(row_of(b), BLOCK)
        total = base[rows, :] + acc[pl.ds(pl.multiple_of(b * BLOCK, BLOCK), BLOCK), :]
        high = total.astype(jnp.bfloat16)
        out_ref[0, rows, :] = high
        return rows, high, (total - high.astype(jnp.float32)).astype(jnp.bfloat16)

    def finish_near(begin, end):
        @pl.loop(begin // BLOCK, end // BLOCK)
        def _(b):
            rows, _, rest = finish(b)
            low[rows, :] = rest

    for q in range(2):
        differences(q)
        sent.append(send(ring[q], ring[14 + q], z_send.at[q], z_recv.at[q], (vir_at(0, 1, 0), occ)))
        pass_on(0, 0, q)
    for q in range(2):
        deal_step(0, 0, q)
    for load in loads[3:]:
        load.wait()

    for h, step in ((0, 1), (0, 2), (1, 0), (0, 3), (1, 1), (1, 2), (1, 3)):
        by_ring = range(1) if (h, step) == (1, 3) else range(2)
        for q in by_ring:
            await_step(h, step, q)
            if step < 3 and not (h == 1 and step == 2 and q == 1):
                pass_on(h, step, q)
            if step == 3:
                deal_step(h, step, q)
        if step < 3:
            for q in range(2):
                deal_step(h, step, q)
        if (h, step) == (0, 1):
            prepare_projector()
        elif (h, step) == (0, 2):
            for i in range(4):
                prepare_base(i)
        elif (h, step) == (1, 0):
            for l in range(SLOTS):
                prepare_ladder(l)
        elif (h, step) == (0, 3):
            multiply(0, NEAR, 0)
        elif (h, step) == (1, 1):
            multiply(NEAR, ROWS, 0)
        elif (h, step) == (1, 2):
            multiply(0, EARLY, 1)
            finish_near(0, EARLY)

    multiply(EARLY, NEAR, 1)
    finish_near(EARLY, NEAR)
    near[...] = jnp.dot(proj_t[...], out_ref[0], preferred_element_type=jnp.float32) + jnp.dot(
        proj_t[...], low[...], preferred_element_type=jnp.float32
    )
    multiply(NEAR, ROWS, 1)

    @pl.loop(0, LAST // BLOCK)
    def _(i):
        _, high, _ = finish(NEAR // BLOCK + i)
        rows = pl.ds(pl.multiple_of(i * BLOCK, BLOCK), BLOCK)
        last[rows, :] = high

    both = (
        near[...]
        + jnp.dot(proj_last[...], last[...], preferred_element_type=jnp.float32)
    )
    for o in range(NO):
        mine = both[PAD * o : PAD * (o + 1), :]
        rest = [mine[4 * m : 4 * (m + 1), FOLD:] for m in range(3)]
        part[o] = jnp.concatenate(
            [mine[0:SHARE, 0:FOLD], jnp.concatenate(rest, axis=1)], axis=0
        ).astype(jnp.bfloat16)

    @pl.loop(1, NO)
    def _(j):
        to = lax.rem(occ + j, NO)
        send(part.at[to], got.at[j - 1], o_send, o_recv, (vir, to))

    for copy in sent:
        copy.wait_send()
    for q in range(2):
        arrived = chunks[q].at[0 : TILES - 1]
        pltpu.make_async_copy(arrived, arrived, p1_send.at[q]).wait()
    for i in range(28):
        dealt = across[i // 2 - 12] if i in (25, 27) else picked[i]
        pltpu.make_async_copy(dealt, dealt, x_send.at[i]).wait()
    for i in range(8):
        h, way, q = i // 4, (i // 2) % 2, i % 2
        dealt = far[h * 2 + q].at[way]
        pltpu.make_async_copy(dealt, dealt, far_send.at[i]).wait()
    arrival(got, o_recv)
    total = part[occ].astype(jnp.float32)
    for j in range(NO - 1):
        total = total + got[j].astype(jnp.float32)
    out2_ref[:, 0, 0:FOLD] = total[0:SHARE, :]
    for m in range(3):
        out2_ref[4 * m : 4 * (m + 1), 0, FOLD:] = total[SHARE:, 128 * m : 128 * (m + 1)]

    pltpu.make_async_copy(got, got, o_send).wait()


def on_device(
    triple_amps, double_amps, ladder_block_table, source_ids, list_length, partner, virtual_energy,
    triple_occupied_energy, coupling, projector,
):
    vmem, hbm = pl.BlockSpec(memory_space=pltpu.VMEM), pl.BlockSpec(memory_space=pltpu.HBM)
    bf16, f32, i32 = jnp.bfloat16, jnp.float32, jnp.int32
    dma = pltpu.SemaphoreType.DMA
    arrays = (
        triple_amps, double_amps, ladder_block_table, source_ids.T, list_length, partner, virtual_energy,
        triple_occupied_energy.reshape(1, ROWS), coupling.T, projector.T,
    )
    sigma_triples, sigma_doubles = pl.pallas_call(
        kernel,
        out_shape=(
            jax.ShapeDtypeStruct((1, ROWS, COLS), bf16),
            jax.ShapeDtypeStruct((SHARE, 1, COLS), f32),
        ),
        in_specs=[hbm] * len(arrays),
        out_specs=(vmem, vmem),
        scratch_shapes=[
            pltpu.VMEM((ROWS, COLS), bf16),
            pltpu.VMEM((OCCJ, COLS), bf16),
            pltpu.SMEM((SLOTS, TILES), i32),
            pltpu.SMEM((TILES,), i32),
            pltpu.SMEM((TILES,), i32),
            pltpu.VMEM((1, COLS), f32),
            pltpu.VMEM((1, ROWS), f32),
            pltpu.VMEM((OCCJ, ROWS), bf16),
            pltpu.VMEM((OCCJ, ROWS), bf16),
            pltpu.VMEM((SLOTS, COLS, COLS), bf16),
            [pltpu.VMEM((TILES, BLOCK, QUARTER), bf16)] * 2,
            [pltpu.VMEM((PAIRS, BLOCK, QUARTER), bf16)] * 28,
            [pltpu.VMEM((NX - 1, BLOCK, SLOTS * QUARTER), bf16)] * 28,
            [pltpu.VMEM((NX, BLOCK, SLOTS * QUARTER), bf16)] * 2,
            [pltpu.VMEM((2, NX, BLOCK, THIRD * QUARTER), bf16)] * 4,
            pltpu.VMEM((2 * NZ, ROWS, SLOTS * QUARTER), bf16),
            pltpu.VMEM((2 * NZ, SLOTS * QUARTER, COLS), bf16),
            pltpu.VMEM((ROWS, COLS), f32),
            pltpu.VMEM((ROWS, COLS), f32),
            pltpu.VMEM((ROWS, COLS), bf16),
            pltpu.VMEM((LAST, COLS), bf16),
            pltpu.VMEM((NO * PAD, COLS), f32),
            pltpu.VMEM((NO * PAD, ROWS), bf16),
            pltpu.VMEM((NO * PAD, LAST), bf16),
            pltpu.VMEM((NO, PAD, FOLD), bf16),
            pltpu.VMEM((NO - 1, PAD, FOLD), bf16),
            pltpu.SMEM((TILES,), jnp.int32),
            pltpu.SMEM((TILES + 1,), jnp.int32),
            pltpu.SMEM((PAIRS,), jnp.int32),
            pltpu.SMEM((4 * NX * SLOTS,), jnp.int32),
            dma((10,)), dma((2,)), dma((2,)), dma((2,)), dma((2,)), dma((2,)),
            dma((24,)), dma((24,)), dma((28,)), dma((32,)), dma((8,)),
            dma, dma,
        ],
        compiler_params=pltpu.CompilerParams(
            collective_id=0, has_side_effects=True, vmem_limit_bytes=48 * 1024 * 1024
        ),
        name="sigma",
    )(*(pltpu.with_memory_space_constraint(a, pltpu.HBM) for a in arrays))
    return sigma_triples, jnp.swapaxes(sigma_doubles, 0, 1)


def solution(mesh):
    return jax.shard_map(
        on_device,
        mesh=mesh,
        in_specs=(
            P("vir", "occ", None),
            P("vir", None, None),
            P("vir", None, None, None),
            P(),
            P(),
            P(),
            P("vir", None),
            P("occ"),
            P("occ", None),
            P("occ", None),
        ),
        out_specs=(P("vir", "occ", None), P("vir", "occ", None)),
        check_vma=False,
    )
```
